256 devices in a mesh: tm: 8 (over z), spec: 32 (over x, y, core).
Axes of the slice: x: 4, y: 4, z: 8, core: 2. Of those that a mesh axis runs over, the one named last changes fastest.
Arguments:
- base_flow: float32 [8, 2048, 2048], P('tm', 'spec'), may hold values from -6 to 6
- tangents: float32 [8, 2, 2048, 2048], P('tm', None, 'spec'), as said below
- end_matrix: float32 [2, 2], replicated, may hold values from 0.5 to 1.5
Outputs:
- covariant_vectors: float32 [8, 2, 2048, 2048], P('tm', None, 'spec')
- evolved_basis: float32 [8, 2, 2048, 2048], P('tm', None, 'spec')
- coefficients: float32 [8, 2, 2], P('tm')
- growth: float32 [8, 2], P('tm')
The draws below stay inside these ranges and needn't reach their ends.
Inputs may be any that keep to these rules, and one draw needn't show every extreme that they name: `tangents`: real values.
All inputs are finite; a program needn't handle non-finite values.
Results may differ from the reference program's by a relative error of at most 0.025.
Values sent between devices are 32-bit elements; how exact they have to be, the bound alone decides.
A program may use at most 128 MiB of HBM per device.

```python
import math
import jax
import jax.numpy as jnp
from jax import lax

NG = 2048
K = 2
SEG = 8


def draw_tangents(key, part):
    white_key, scale_key, mix_key = jax.random.split(jax.random.fold_in(key, 17), 3)
    independent = jax.random.truncated_normal(white_key, -6.0, 6.0, (SEG, K, NG, NG), jnp.float32)
    scales = jnp.exp(jax.random.uniform(scale_key, (SEG, K), jnp.float32, math.log(0.5), math.log(4.0)))
    mixing = jnp.tril(jax.random.normal(mix_key, (SEG, K, K), jnp.float32) * 0.6, -1)
    mixing = mixing + jnp.eye(K, dtype=jnp.float32)[None] * scales[:, :, None]
    return jnp.einsum('sij,sjab->siab', mixing, independent).astype(jnp.float32)


def block_levels(rng, extent, cuts, smallest, high):
    loudness, own = 1.0, jax.random.fold_in(rng, 6)
    for dim, parts in cuts:
        heights = jnp.exp(jax.random.uniform(jax.random.fold_in(own, dim), (parts,), jnp.float32, smallest / len(cuts), high / len(cuts)))
        loudness = loudness * jnp.repeat(heights, extent[dim] // parts).reshape([-1 if axis == dim else 1 for axis in range(len(extent))])
    return loudness


def normal_values(key, extent, scale, most, pieces=(), kind=jnp.bfloat16):
    gain = block_levels(key, extent, pieces, -0.22, 0.18) if pieces else 1.0
    drawn = jax.random.normal(key, extent, jnp.float32) * scale * gain
    return jnp.minimum(jnp.maximum(drawn, -most), most).astype(kind)


def setup_inputs(seed: int = 0) -> dict:
    seeds = jax.random.split(jax.random.key(seed), 4)
    return {
        "base_flow": normal_values(seeds[0], (SEG, NG, NG), 1.0, 6.0, ((0, 8), (1, 32)), jnp.float32),
        "tangents": draw_tangents(jax.random.fold_in(seeds[3], 71), 0),
        "end_matrix": jnp.clip(jax.random.uniform(seeds[2], (K, K), jnp.float32, 0.5, 1.5), 0.5, 1.5),
    }


time_step = 0.1
visc_scale = 15.0
precise = lax.Precision.HIGHEST

def wave_tables():
    band_limit = NG // 3
    first_index = jnp.arange(NG, dtype=jnp.int32)
    first_signed = jnp.where(first_index < NG // 2, first_index, first_index - NG)
    second_index = jnp.arange(NG // 2 + 1, dtype=jnp.int32)
    keep_mask = ((jnp.abs(first_signed)[:, None] <= band_limit) & (second_index[None, :] <= band_limit)).astype(jnp.float32)
    first_wave = first_signed.astype(jnp.float32)[:, None]
    second_wave = second_index.astype(jnp.float32)[None, :]
    wave_square = first_wave * first_wave + second_wave * second_wave
    inverse_square = jnp.where(wave_square > 0.0, 1.0 / jnp.maximum(wave_square, 1.0), 0.0)
    decay_factor = jnp.exp(-(visc_scale / band_limit ** 2) * time_step * wave_square)
    return (first_wave, second_wave, keep_mask, inverse_square, decay_factor)

def to_spectrum(fields, tables):
    return jnp.fft.rfft2(fields) * tables[2]

def to_fields(spectrum):
    return jnp.fft.irfft2(spectrum, s=(NG, NG))

def flow_terms(spectrum, tables):
    first_wave, second_wave, keep_mask, inverse_square, decay_factor = tables
    potential = spectrum * inverse_square
    return (to_fields(1j * first_wave * spectrum), to_fields(1j * second_wave * spectrum), to_fields(1j * second_wave * potential), to_fields(-1j * first_wave * potential))

def tangent_terms(flow_fields):
    gradient_first, gradient_second, velocity_first, velocity_second = flow_fields
    return -(velocity_first[:1] * gradient_first[1:] + velocity_second[:1] * gradient_second[1:] + velocity_first[1:] * gradient_first[:1] + velocity_second[1:] * gradient_second[:1])

def one_segment(inputs):
    base_slice, tangent_slice = inputs
    tables = wave_tables()
    decay_factor = tables[4]
    fields = jnp.concatenate([base_slice[None], tangent_slice], axis=0)
    start_spectrum = to_spectrum(fields, tables)
    slope_spectrum = to_spectrum(tangent_terms(flow_terms(start_spectrum, tables)), tables)
    final_spectrum = decay_factor * (start_spectrum[1:] + time_step * slope_spectrum)
    evolved = to_fields(final_spectrum)
    gram_matrix = jnp.einsum('iab,jab->ij', evolved, evolved, precision=precise) / (NG * NG)
    upper_factor = jnp.linalg.cholesky(gram_matrix).T
    growth = jnp.log(jnp.diagonal(upper_factor))
    inverse_upper = lax.linalg.triangular_solve(upper_factor, jnp.eye(K, dtype=jnp.float32), left_side=True, lower=False)
    evolved_basis = jnp.einsum('ij,iab->jab', inverse_upper, evolved, precision=precise)
    return (inverse_upper, growth, evolved_basis)

def reference(base_flow, tangents, end_matrix):
    inverse_uppers, growth, evolved_basis = lax.map(one_segment, (base_flow, tangents))
    identity = jnp.eye(K, dtype=jnp.float32)
    later_list = [identity]
    for segment in range(SEG - 1, 0, -1):
        later_list.append(jnp.dot(inverse_uppers[segment], later_list[-1], precision=precise))
    later_list = later_list[::-1]
    upper_part = jnp.triu(end_matrix)
    coefficient_list = []
    for segment in range(SEG):
        raw_product = jnp.dot(jnp.dot(inverse_uppers[segment], later_list[segment], precision=precise), upper_part, precision=precise)
        column_norm = jnp.sqrt(lax.optimization_barrier(jnp.sum(raw_product * raw_product, axis=0, keepdims=True)))
        coefficient_list.append(raw_product / column_norm)
    coefficients = jnp.stack(coefficient_list)
    covariant_vectors = jnp.einsum('sij,siab->sjab', coefficients, tangents, precision=precise)
    return (covariant_vectors, evolved_basis, coefficients, growth)
```

```python
import functools
import math

import jax
import jax.numpy as jnp
import ml_dtypes
import numpy as np
from jax import lax
from jax.experimental import pallas as pl
from jax.experimental.pallas import tpu as pltpu
from jax.sharding import PartitionSpec as P

NG = 2048
HALF = NG // 2
K = 2
SPEC = 32
TM = 8
SLAB = NG // SPEC
BAND = NG // 3
ROWS = 22
PAD = 24
LANES = 128
SIDE = 16 * 2 * PAD

time_step = 0.1
visc_scale = 15.0
MESH = pl.DeviceIdType.MESH
F32 = jnp.float32
BF16 = jnp.bfloat16


def row_tables():
    owner = np.arange(16)[:, None, None]
    part = np.arange(2)[None, :, None]
    row = np.arange(PAD)[None, None, :]
    y = np.arange(HALF)[None, :]
    tables = []
    for parity in range(2):
        wave = 2 * (ROWS * owner + row) + parity
        valid = np.broadcast_to((wave <= BAND) & (row < ROWS), (16, 2, PAD)).reshape(SIDE, 1)
        waves = np.broadcast_to(wave, (16, 2, PAD)).reshape(SIDE, 1)
        parts = np.broadcast_to(part, (16, 2, PAD)).reshape(SIDE, 1)
        angle = (waves * y % NG) * (2.0 * math.pi / NG)
        tables.append(np.where(valid, np.where(parts == 0, np.cos(angle), -np.sin(angle)), 0.0))
    return np.stack(tables)


def lane_tables():
    index = np.arange(SLAB)
    angle = (index[:, None] * index[None, :] % SLAB) * (2.0 * math.pi / SLAB)
    cos, sin, zero = np.cos(angle), np.sin(angle), np.zeros((SLAB, SLAB))
    pair_forward = np.block(
        [[cos, zero, -sin, zero], [zero, cos, zero, -sin], [sin, zero, cos, zero], [zero, sin, zero, cos]]
    )
    pair_inverse = np.block(
        [[cos, zero, sin, zero], [zero, cos, zero, sin], [-sin, zero, cos, zero], [zero, -sin, zero, cos]]
    )
    twice = []
    for half in range(2):
        real = pair_forward[:, half * SLAB : (half + 1) * SLAB]
        imag = pair_forward[:, (2 + half) * SLAB : (3 + half) * SLAB]
        twice.append(np.concatenate([imag, imag, -real, -real], axis=1))
    return np.stack([twice[0], twice[1], pair_forward, pair_inverse])


def twist_tables():
    first = np.arange(32)[:, None]
    place = (np.arange(LANES) % SLAB)[None, :]
    angle = (first * place) * (2.0 * math.pi / NG)
    return np.stack([np.cos(angle), np.sin(angle)])


def turned(re, im, angle):
    c, s = math.cos(angle), math.sin(angle)
    if abs(s) < 1e-9 and c > 0:
        return re, im
    if abs(c) < 1e-9:
        return (-im, re) if s > 0 else (im, -re)
    if abs(abs(c) - abs(s)) < 1e-9:
        root = math.sqrt(0.5)
        sc, ss = (root if c > 0 else -root), (root if s > 0 else -root)
        if sc == ss:
            return (re - im) * sc, (re + im) * sc
        return (re + im) * sc, (im - re) * sc
    return re * c - im * s, re * s + im * c


def short_transform(res, ims, sign):
    count = len(res)
    if count == 1:
        return res, ims
    er, ei = short_transform(res[0::2], ims[0::2], sign)
    dr, di = short_transform(res[1::2], ims[1::2], sign)
    half = count // 2
    out_r, out_i = [None] * count, [None] * count
    for k in range(half):
        tr, ti = turned(dr[k], di[k], sign * 2.0 * math.pi * k / count)
        out_r[k], out_i[k] = er[k] + tr, ei[k] + ti
        out_r[k + half], out_i[k + half] = er[k] - tr, ei[k] - ti
    return out_r, out_i


def dot(a, b):
    return jnp.dot(a, b, preferred_element_type=F32)


def kernel(
    base_ref,
    tang_ref,
    end_ref,
    tf_ref,
    ti_ref,
    lane_ref,
    twist_ref,
    cov_ref,
    basis_ref,
    coef_ref,
    growth_ref,
    s1,
    r1,
    s2,
    r2,
    s3,
    r3,
    s4,
    r4,
    gs,
    gr,
    ts,
    tr,
    tb,
    tt,
    tw,
    folded,
    zr,
    zi,
    mult_flow,
    mult_slope,
    mult_decay,
    base_flow,
    product,
    send_sem,
    recv_sem,
):
    me = lax.axis_index("spec")
    seg = lax.axis_index("tm")
    my_slot = lax.rem(me, 2) * 16 + me // 2
    low = lax.broadcasted_iota(jnp.int32, (1, LANES), 1) < SLAB

    barrier = pltpu.get_barrier_semaphore()

    def greet(d, carry):
        pl.semaphore_signal(barrier, inc=1, device_id={"spec": lax.rem(me + d, SPEC)}, device_id_type=MESH)
        return carry

    for ref in (r1, r2, r3, r4):
        lead = ref.shape[:-2]
        ref[(slice(None),) * len(lead) + (slice(16, 24), slice(None))] = jnp.zeros(lead + (8, LANES), F32)

    lax.fori_loop(1, SPEC, greet, 0)

    def greet_segment(d, carry):
        pl.semaphore_signal(barrier, inc=1, device_id={"tm": lax.rem(seg + d, TM)}, device_id_type=MESH)
        return carry

    lax.fori_loop(1, TM, greet_segment, 0)

    def send_all(phase, source, target):
        def step(d, carry):
            peer = lax.rem(me + d, SPEC)
            slot = lax.rem(peer, 2) * 16 + peer // 2
            pltpu.make_async_remote_copy(
                src_ref=source(peer, slot),
                dst_ref=target,
                send_sem=send_sem.at[phase],
                recv_sem=recv_sem.at[phase],
                device_id={"spec": peer},
                device_id_type=MESH,
            ).start()
            return carry

        lax.fori_loop(1, SPEC, step, 0)

    def wait_for(sem, phase, ref):
        pltpu.make_async_copy(ref, ref, sem.at[phase]).wait()

    some = pl.ds(0, ROWS)
    most = pl.ds(0, SPEC - 1)

    for parity in range(2):
        def fold(half_parity=parity):
            for index, ref in ((0, tang_ref.at[0, 0]), (1, tang_ref.at[0, 1]), (2, base_ref.at[0]), (3, base_ref.at[0])):
                lo, hi = ref[:, :HALF], ref[:, HALF:]
                value = lo + hi if half_parity == 0 else lo - hi
                folded[index * SLAB : (index + 1) * SLAB, :] = value.astype(BF16)

        fold()

        def spectrum_rows(step, carry, parity=parity):
            rows = pl.ds(pl.multiple_of(step * 192, 192), 192)
            out = lax.dot_general(
                tf_ref[parity, rows, :], folded[...], (((1,), (1,)), ((), ())), preferred_element_type=F32
            ).reshape(4, 2, PAD, 2 * LANES)
            slots = pl.ds(parity * 16 + step * 4, 4)
            s1[slots, 0] = jnp.where(low[None], out[:, 0, :, LANES:], out[:, 1, :, LANES:])
            s1[slots, 1] = out[:, 0, :, :LANES]
            s1[slots, 2] = out[:, 1, :, :LANES]
            return carry

        lax.fori_loop(0, 4, spectrum_rows, 0)

    pl.semaphore_wait(barrier, SPEC - 1 + TM - 1)
    send_all(0, lambda peer, slot: s1.at[slot, pl.ds(0, 1), some], r1.at[me, pl.ds(0, 1), some])
    send_all(1, lambda peer, slot: s1.at[slot, pl.ds(1, 2), some], r1.at[me, pl.ds(1, 2), some])
    r1[me] = s1[my_slot]

    lane = lax.broadcasted_iota(jnp.int32, (PAD, LANES), 1)
    row = lax.broadcasted_iota(jnp.int32, (PAD, LANES), 0)
    second = 2 * (ROWS * (me // 2) + row) + lax.rem(me, 2)
    second_keep = (second <= BAND) & (row < ROWS)
    second_wave = second.astype(F32)
    low_rows = lane < SLAB
    column = jnp.where(second == 0, 1.0, 2.0)
    to_field = column * (1.0 / float(NG * NG))
    gram_weight = jnp.where(second_keep, column * (1.0 / float(NG) ** 4), 0.0)

    def multipliers(k1, carry):
        first = k1 + 32 * lax.rem(lane, SLAB)
        first = jnp.where(first < HALF, first, first - NG)
        first_wave = first.astype(F32)
        keep = jnp.where(second_keep & (jnp.abs(first) <= BAND), 1.0, 0.0)
        square = first_wave * first_wave + second_wave * second_wave
        inverse = jnp.where(square > 0.0, 1.0 / jnp.maximum(square, 1.0), 0.0)
        decay = keep * jnp.exp(-(visc_scale / BAND**2) * time_step * square)
        mult_flow[k1] = keep * to_field * inverse * jnp.where(low_rows, -second_wave, first_wave)
        mult_decay[k1] = decay
        mult_slope[k1] = (time_step * decay) * jnp.where(
            low_rows,
            first_wave * first_wave - second_wave * second_wave,
            2.0 * first_wave * second_wave,
        )
        return carry

    lax.fori_loop(0, 32, multipliers, 0)

    def first_forward(load, target):
        def body(step, carry):
            rows = pl.ds(pl.multiple_of(step * 8, 8), 8)
            pairs = [load(i, rows) for i in range(SPEC)]
            re, im = short_transform([p[0] for p in pairs], [p[1] for p in pairs], -1.0)
            for k1 in range(32):
                c, s = twist_ref[0, k1 : k1 + 1, :], twist_ref[1, k1 : k1 + 1, :]
                target[k1, rows, :LANES] = re[k1] * c + im[k1] * s
                target[k1, rows, LANES:] = im[k1] * c - re[k1] * s
            return carry

        lax.fori_loop(0, PAD // 8, body, 0)

    def first_inverse(target):
        def body(step, carry):
            rows = pl.ds(pl.multiple_of(step * 8, 8), 8)
            res, ims = [], []
            for k1 in range(32):
                c, s = twist_ref[0, k1 : k1 + 1, :], twist_ref[1, k1 : k1 + 1, :]
                re, im = tw[k1, rows, :LANES], tw[k1, rows, LANES:]
                res.append(re * c - im * s)
                ims.append(im * c + re * s)
            re, im = short_transform(res, ims, 1.0)
            for i in range(SPEC):
                target[i, 0, rows, :] = re[i]
                target[i, 1, rows, :] = im[i]
            return carry

        lax.fori_loop(0, PAD // 8, body, 0)

    def chunks(body):
        def step(c, carry):
            body(pl.ds(c * 8, 8))
            return carry

        lax.fori_loop(0, 4, step, 0)

    def flow(source, which, index):
        def body(part):
            spectrum = dot(source[part].reshape(192, 256).astype(BF16), lane_ref[which])
            factor = mult_flow[part].reshape(192, LANES)
            scaled = jnp.concatenate([spectrum[:, :LANES] * factor, spectrum[:, LANES:] * factor], axis=1)
            tw[part] = dot(scaled.astype(BF16), lane_ref[3]).reshape(8, PAD, 256)

        chunks(body)
        first_inverse(s2.at[index])
        send_all(2 + index, lambda peer, slot: s2.at[index, peer, :, some], r2.at[index, my_slot, :, some])
        r2[index, my_slot] = s2[index, me]

    sign = jnp.where(low, 1.0, -1.0)

    def load_base(i, rows):
        value = r1[i, 0, rows, :]
        return value, pltpu.roll(value, SLAB, 1) * sign

    wait_for(recv_sem, 0, r1.at[most, pl.ds(0, 1), some])
    first_forward(load_base, tb)
    flow(tb, 0, 0)
    wait_for(recv_sem, 1, r1.at[most, pl.ds(1, 2), some])
    first_forward(lambda i, rows: (r1[i, 1, rows, :], r1[i, 2, rows, :]), tt)
    flow(tt, 0, 1)
    flow(tt, 1, 2)

    def start_spectrum(part):
        spectrum = dot(tt[part].reshape(192, 256).astype(BF16), lane_ref[2])
        decay = mult_decay[part]
        zr[part] = spectrum[:, :LANES].reshape(8, PAD, LANES) * decay
        zi[part] = spectrum[:, LANES:].reshape(8, PAD, LANES) * decay

    chunks(start_spectrum)

    def second_inverse(ref, body):
        even = ref[pl.ds(0, 16)].reshape(SIDE, LANES).astype(BF16)
        odd = ref[pl.ds(16, 16)].reshape(SIDE, LANES).astype(BF16)

        def step(c, carry):
            rows = pl.ds(pl.multiple_of(c * 256, 256), 256)
            e = dot(ti_ref[0, rows, :], even)
            o = dot(ti_ref[1, rows, :], odd)
            body(c, e + o, e - o)
            return carry

        lax.fori_loop(0, 4, step, 0)

    wait_for(recv_sem, 2, r2.at[0, most, :, some])

    def keep_base(c, lower, upper):
        base_flow[pl.ds(pl.multiple_of(c * 256, 256), 256), :] = lower
        base_flow[pl.ds(pl.multiple_of(c * 256 + HALF, 256), 256), :] = upper

    second_inverse(r2.at[0], keep_base)

    def products(b, t):
        straight = b * t
        crossed = b * pltpu.roll(t, SLAB, 1)
        near = jnp.where(low, crossed, straight)
        far = pltpu.roll(jnp.where(low, straight, crossed), SLAB, 1)
        return near + far * sign

    for index in range(2):
        wait_for(recv_sem, 3 + index, r2.at[1 + index, most, :, some])

        def multiply(c, lower, upper):
            rows = pl.ds(pl.multiple_of(c * 256, 256), 256)
            lo = products(base_flow[rows, :], lower)
            hi = products(base_flow[pl.ds(pl.multiple_of(c * 256 + HALF, 256), 256), :], upper)
            product[0, rows, :] = (lo + hi).astype(BF16)
            product[1, rows, :] = (lo - hi).astype(BF16)

        second_inverse(r2.at[1 + index], multiply)

        for parity in range(2):
            def product_rows(step, carry, parity=parity, index=index):
                rows = pl.ds(pl.multiple_of(step * 192, 192), 192)
                out = dot(tf_ref[parity, rows, :], product[parity])
                s3[index, pl.ds(parity * 16 + step * 4, 4)] = out.reshape(4, 2, PAD, LANES)
                return carry

            lax.fori_loop(0, 4, product_rows, 0)

        send_all(
            5 + index,
            lambda peer, slot, index=index: s3.at[index, slot, :, some],
            r3.at[index, me, :, some],
        )
        r3[index, me] = s3[index, my_slot]

    for index in range(2):
        wait_for(recv_sem, 5 + index, r3.at[index, most, :, some])
        first_forward(lambda i, rows, index=index: (r3[index, i, 0, rows, :], r3[index, i, 1, rows, :]), tb)

        def add_slope(part, index=index):
            spectrum = dot(tb[part].reshape(192, 256).astype(BF16), lane_ref[2])
            factor = mult_slope[part].reshape(192, LANES)
            for half, ref in ((0, zr), (1, zi)):
                terms = spectrum[:, half * LANES : (half + 1) * LANES] * factor
                slope = terms + pltpu.roll(terms, SLAB, 1)
                slope = jnp.where(low, slope, 0.0) if index == 0 else jnp.where(low, 0.0, slope)
                ref[part] = ref[part] + slope.reshape(8, PAD, LANES)

        chunks(add_slope)

    def inner(k1, carry):
        squares, crosses = carry
        re, im = zr[k1], zi[k1]
        squares = squares + (re * re + im * im) * gram_weight
        crosses = crosses + (re * pltpu.roll(re, SLAB, 1) + im * pltpu.roll(im, SLAB, 1)) * gram_weight
        return squares, crosses

    nothing = jnp.zeros((PAD, LANES), F32)
    squares, crosses = lax.fori_loop(0, 32, inner, (nothing, nothing))

    def total(x):
        return jnp.sum(jnp.sum(x, axis=0, keepdims=True), axis=1, keepdims=True)

    lane8 = lax.broadcasted_iota(jnp.int32, (8, LANES), 1)

    def spread(first, second, third):
        return jnp.where(lane8 == 0, first, jnp.where(lane8 == 1, second, jnp.where(lane8 == 2, third, 0.0)))

    g00 = total(jnp.where(low_rows, squares, 0.0))
    g11 = total(jnp.where(low_rows, 0.0, squares))
    g01 = total(jnp.where(low_rows, crosses, 0.0))
    gs[...] = spread(g00, g01, g11)
    send_all(8, lambda peer, slot: gs, gr.at[me])
    gr[me] = gs[...]

    def final_chunk(part):
        scale = jnp.broadcast_to(to_field[None], (8, PAD, LANES))
        scaled = jnp.concatenate(
            [(zr[part] * scale).reshape(192, LANES), (zi[part] * scale).reshape(192, LANES)], axis=1
        )
        tw[part] = dot(scaled.astype(BF16), lane_ref[3]).reshape(8, PAD, 256)

    chunks(final_chunk)
    first_inverse(s4)
    send_all(7, lambda peer, slot: s4.at[peer, :, some], r4.at[my_slot, :, some])
    r4[my_slot] = s4[me]

    def pick(values, index):
        return jnp.sum(jnp.where(lane8[:1] == index, values, 0.0), axis=1, keepdims=True)

    wait_for(recv_sem, 8, gr.at[most])
    gram = jnp.sum(gr[...], axis=0)[:1]
    g00, g01, g11 = pick(gram, 0), pick(gram, 1), pick(gram, 2)
    u00 = jnp.sqrt(g00)
    u01 = g01 / u00
    u11 = jnp.sqrt(g11 - u01 * u01)
    i00, i11 = 1.0 / u00, 1.0 / u11
    i01 = -(i00 * u01) / u11
    i10 = jnp.zeros_like(i00)
    ts[...] = spread(i00, i01, i11)

    def share(d, carry):
        pltpu.make_async_remote_copy(
            src_ref=ts,
            dst_ref=tr.at[seg],
            send_sem=send_sem.at[9],
            recv_sem=recv_sem.at[9],
            device_id={"tm": lax.rem(seg + d, TM)},
            device_id_type=MESH,
        ).start()
        return carry

    lax.fori_loop(1, TM, share, 0)
    tr[seg] = ts[...]
    pair = lax.broadcasted_iota(jnp.int32, (1, 2), 1)
    growth_ref[...] = jnp.where(pair == 0, jnp.log(u00), jnp.log(u11))

    wait_for(recv_sem, 9, tr.at[pl.ds(0, TM - 1)])
    one, zero = jnp.ones_like(i00), jnp.zeros_like(i00)
    end00, end01, end11 = end_ref[0, 0], end_ref[0, 1], end_ref[1, 1]
    p00, p01, p10, p11 = one, zero, zero, one
    for later in range(TM - 1, -1, -1):
        values = tr[later][:1]
        active = later >= seg
        a00 = jnp.where(active, pick(values, 0), one)
        a01 = jnp.where(active, pick(values, 1), zero)
        a11 = jnp.where(active, pick(values, 2), one)
        a10 = zero
        p00, p01, p10, p11 = (
            a00 * p00 + a01 * p10,
            a00 * p01 + a01 * p11,
            a10 * p00 + a11 * p10,
            a10 * p01 + a11 * p11,
        )
    q00, q01 = p00 * end00, p00 * end01 + p01 * end11
    q10, q11 = p10 * end00, p10 * end01 + p11 * end11
    norm0 = jnp.sqrt(q00 * q00 + q10 * q10)
    norm1 = jnp.sqrt(q01 * q01 + q11 * q11)
    c00, c10, c01, c11 = q00 / norm0, q10 / norm0, q01 / norm1, q11 / norm1
    across = lax.broadcasted_iota(jnp.int32, (2, 2), 1)
    down = lax.broadcasted_iota(jnp.int32, (2, 2), 0)
    coef_ref[0] = jnp.where(
        down == 0, jnp.where(across == 0, c00, c01), jnp.where(across == 0, c10, c11)
    )
    cov_ref[0, 0] = tang_ref[0, 0] * c00 + tang_ref[0, 1] * c10
    cov_ref[0, 1] = tang_ref[0, 0] * c01 + tang_ref[0, 1] * c11

    wait_for(recv_sem, 7, r4.at[most, :, some])
    even = r4[pl.ds(0, 16)].reshape(SIDE, LANES).T.astype(BF16)
    odd = r4[pl.ds(16, 16)].reshape(SIDE, LANES).T.astype(BF16)
    for c in range(4):
        e = dot(even, tf_ref[0, :, c * 256 : (c + 1) * 256])
        o = dot(odd, tf_ref[1, :, c * 256 : (c + 1) * 256])
        for start, value in ((c * 256, e + o), (c * 256 + HALF, e - o)):
            first, second_value = value[:SLAB], value[SLAB:]
            basis_ref[0, 0, :, start : start + 256] = first * i00 + second_value * i10
            basis_ref[0, 1, :, start : start + 256] = first * i01 + second_value * i11

    wait_for(send_sem, 0, s1.at[most, pl.ds(0, 1), some])
    wait_for(send_sem, 1, s1.at[most, pl.ds(1, 2), some])
    for index in range(3):
        wait_for(send_sem, 2 + index, s2.at[index, most, :, some])
    for index in range(2):
        wait_for(send_sem, 5 + index, s3.at[index, most, :, some])
    wait_for(send_sem, 7, s4.at[most, :, some])
    wait_for(send_sem, 8, gr.at[most])
    wait_for(send_sem, 9, tr.at[pl.ds(0, TM - 1)])


def shards(base_flow, tangents, end_matrix):
    rows = row_tables()
    tf = jnp.asarray(rows.astype(ml_dtypes.bfloat16))
    ti = jnp.asarray(np.ascontiguousarray(rows.transpose(0, 2, 1)).astype(ml_dtypes.bfloat16))
    lanes = jnp.asarray(lane_tables().astype(ml_dtypes.bfloat16))
    twist = jnp.asarray(twist_tables().astype(np.float32))
    vmem = pl.BlockSpec(memory_space=pltpu.VMEM)
    smem = pl.BlockSpec(memory_space=pltpu.SMEM)

    def buffer(*lead):
        return pltpu.VMEM(lead + (PAD, LANES), F32)

    return pl.pallas_call(
        kernel,
        out_shape=(
            jax.ShapeDtypeStruct((1, K, SLAB, NG), F32),
            jax.ShapeDtypeStruct((1, K, SLAB, NG), F32),
            jax.ShapeDtypeStruct((1, K, K), F32),
            jax.ShapeDtypeStruct((1, K), F32),
        ),
        in_specs=[vmem, vmem, smem, vmem, vmem, vmem, vmem],
        out_specs=(vmem, vmem, vmem, vmem),
        scratch_shapes=[
            buffer(SPEC, 3),
            buffer(SPEC, 3),
            buffer(3, SPEC, 2),
            buffer(3, SPEC, 2),
            buffer(2, SPEC, 2),
            buffer(2, SPEC, 2),
            buffer(SPEC, 2),
            buffer(SPEC, 2),
            pltpu.VMEM((8, LANES), F32),
            pltpu.VMEM((SPEC, 8, LANES), F32),
            pltpu.VMEM((8, LANES), F32),
            pltpu.VMEM((TM, 8, LANES), F32),
            pltpu.VMEM((32, PAD, 256), F32),
            pltpu.VMEM((32, PAD, 256), F32),
            pltpu.VMEM((32, PAD, 256), F32),
            pltpu.VMEM((4 * SLAB, HALF), BF16),
            buffer(32),
            buffer(32),
            buffer(32),
            buffer(32),
            buffer(32),
            pltpu.VMEM((NG, LANES), F32),
            pltpu.VMEM((2, HALF, LANES), BF16),
            pltpu.SemaphoreType.DMA((10,)),
            pltpu.SemaphoreType.DMA((10,)),
        ],
        compiler_params=pltpu.CompilerParams(
            collective_id=0, has_side_effects=True, vmem_limit_bytes=56 * 1024 * 1024
        ),
        cost_estimate=pl.CostEstimate(flops=12_000_000_000, bytes_accessed=12_000_000, transcendentals=0),
    )(base_flow, tangents, end_matrix, tf, ti, lanes, twist)


def solution(mesh):
    in_specs = (P("tm", "spec", None), P("tm", None, "spec", None), P())
    out_specs = (
        P("tm", None, "spec", None),
        P("tm", None, "spec", None),
        P("tm", None, None),
        P("tm", None),
    )
    return jax.shard_map(shards, mesh=mesh, in_specs=in_specs, out_specs=out_specs, check_vma=False)
```

```python
import functools
import math

import jax
import jax.numpy as jnp
import ml_dtypes
import numpy as np
from jax import lax
from jax.experimental import pallas as pl
from jax.experimental.pallas import tpu as pltpu
from jax.sharding import PartitionSpec as P

NG = 2048
HALF = NG // 2
K = 2
SPEC = 32
TM = 8
SLAB = NG // SPEC
BAND = NG // 3
ROWS = 22
PAD = 24
LANES = 128
SIDE = 16 * 2 * PAD

RELAYED = ()
DIRECT = ((2, 2), (1, 2), (2, 1), (3, 2), (2, 3), (2, 0), (0, 2), (1, 1), (3, 3), (1, 3), (3, 1), (1, 0), (0, 1), (3, 0), (0, 3))

time_step = 0.1
visc_scale = 15.0
MESH = pl.DeviceIdType.MESH
F32 = jnp.float32
BF16 = jnp.bfloat16


def row_tables():
    owner = np.arange(16)[:, None, None]
    part = np.arange(2)[None, :, None]
    row = np.arange(PAD)[None, None, :]
    y = np.arange(HALF)[None, :]
    tables = []
    for parity in range(2):
        wave = 2 * (ROWS * owner + row) + parity
        valid = np.broadcast_to((wave <= BAND) & (row < ROWS), (16, 2, PAD)).reshape(SIDE, 1)
        waves = np.broadcast_to(wave, (16, 2, PAD)).reshape(SIDE, 1)
        parts = np.broadcast_to(part, (16, 2, PAD)).reshape(SIDE, 1)
        angle = (waves * y % NG) * (2.0 * math.pi / NG)
        tables.append(np.where(valid, np.where(parts == 0, np.cos(angle), -np.sin(angle)), 0.0))
    return np.stack(tables)


def lane_tables():
    index = np.arange(SLAB)
    angle = (index[:, None] * index[None, :] % SLAB) * (2.0 * math.pi / SLAB)
    cos, sin, zero = np.cos(angle), np.sin(angle), np.zeros((SLAB, SLAB))
    pair_forward = np.block(
        [[cos, zero, -sin, zero], [zero, cos, zero, -sin], [sin, zero, cos, zero], [zero, sin, zero, cos]]
    )
    pair_inverse = np.block(
        [[cos, zero, sin, zero], [zero, cos, zero, sin], [-sin, zero, cos, zero], [zero, -sin, zero, cos]]
    )
    twice = []
    for half in range(2):
        real = pair_forward[:, half * SLAB : (half + 1) * SLAB]
        imag = pair_forward[:, (2 + half) * SLAB : (3 + half) * SLAB]
        twice.append(np.concatenate([imag, imag, -real, -real], axis=1))
    return np.stack([twice[0], twice[1], pair_forward, pair_inverse])


def twist_tables():
    first = np.arange(32)[:, None]
    place = (np.arange(LANES) % SLAB)[None, :]
    angle = (first * place) * (2.0 * math.pi / NG)
    return np.stack([np.cos(angle), np.sin(angle)])


def turned(re, im, angle):
    c, s = math.cos(angle), math.sin(angle)
    if abs(s) < 1e-9 and c > 0:
        return re, im
    if abs(c) < 1e-9:
        return (-im, re) if s > 0 else (im, -re)
    if abs(abs(c) - abs(s)) < 1e-9:
        root = math.sqrt(0.5)
        sc, ss = (root if c > 0 else -root), (root if s > 0 else -root)
        if sc == ss:
            return (re - im) * sc, (re + im) * sc
        return (re + im) * sc, (im - re) * sc
    return re * c - im * s, re * s + im * c


def short_transform(res, ims, sign):
    count = len(res)
    if count == 1:
        return res, ims
    er, ei = short_transform(res[0::2], ims[0::2], sign)
    dr, di = short_transform(res[1::2], ims[1::2], sign)
    half = count // 2
    out_r, out_i = [None] * count, [None] * count
    for k in range(half):
        tr, ti = turned(dr[k], di[k], sign * 2.0 * math.pi * k / count)
        out_r[k], out_i[k] = er[k] + tr, ei[k] + ti
        out_r[k + half], out_i[k + half] = er[k] - tr, ei[k] - ti
    return out_r, out_i


def dot(a, b):
    return jnp.dot(a, b, preferred_element_type=F32)


def kernel(
    base_ref,
    tang_ref,
    end_ref,
    tf_ref,
    ti_ref,
    lane_ref,
    twist_ref,
    even_ref,
    odd_ref,
    small_ref,
    s1,
    r1,
    s2,
    r2,
    s3,
    r3,
    s4,
    r4,
    gs,
    gr,
    ts,
    tr,
    tb,
    tt,
    tw,
    folded,
    zr,
    zi,
    mult_flow,
    mult_slope,
    mult_decay,
    base_flow,
    product,
    landing,
    relay_sem,
    forward_sem,
    send_sem,
    recv_sem,
):
    me = lax.axis_index("spec")
    my_x, my_y, my_core = me // 8, lax.rem(me // 2, 4), lax.rem(me, 2)
    seg = lax.axis_index("tm")
    my_slot = lax.rem(me, 2) * 16 + me // 2
    low = lax.broadcasted_iota(jnp.int32, (1, LANES), 1) < SLAB

    barrier = pltpu.get_barrier_semaphore()

    def greet(d, carry):
        pl.semaphore_signal(barrier, inc=1, device_id={"spec": lax.rem(me + d, SPEC)}, device_id_type=MESH)
        return carry

    for ref in (r1, r2, r3, r4):
        lead = ref.shape[:-2]
        ref[(slice(None),) * len(lead) + (slice(16, 24), slice(None))] = jnp.zeros(lead + (8, LANES), F32)

    lax.fori_loop(1, SPEC, greet, 0)

    def greet_segment(d, carry):
        pl.semaphore_signal(barrier, inc=1, device_id={"tm": lax.rem(seg + d, TM)}, device_id_type=MESH)
        return carry

    lax.fori_loop(1, TM, greet_segment, 0)

    def place(x, y, core):
        return (lax.rem(x, 4) * 4 + lax.rem(y, 4)) * 2 + core

    def slot_of(device):
        return lax.rem(device, 2) * 16 + device // 2

    def start_copy(source, target, out_sem, in_sem, device):
        pltpu.make_async_remote_copy(
            src_ref=source,
            dst_ref=target,
            send_sem=out_sem,
            recv_sem=in_sem,
            device_id={"spec": device},
            device_id_type=MESH,
        ).start()

    def send_core(phase, core, source, target):
        for number, (dx, dy) in enumerate(RELAYED):
            peer = place(my_x + dx, my_y + dy, core)
            start_copy(
                source(peer, slot_of(peer)),
                landing.at[phase, my_core * 2 + number, pl.ds(0, source(0, 0).shape[0]), pl.ds(0, ROWS)],
                send_sem.at[phase],
                relay_sem.at[phase],
                place(my_x, my_y + 2, core),
            )
        for dx, dy in DIRECT:
            peer = place(my_x + dx, my_y + dy, core)
            start_copy(
                source(peer, slot_of(peer)), target(me, my_slot), send_sem.at[phase], recv_sem.at[phase], peer
            )

    def send_other(phase, source, target):
        peer = place(my_x, my_y, 1 - my_core)
        start_copy(
            source(peer, slot_of(peer)), target(me, my_slot), send_sem.at[phase], recv_sem.at[phase], peer
        )

    def send_all(phase, source, target):
        def step(core, carry):
            send_core(phase, core, source, target)
            return carry

        lax.fori_loop(0, 2, step, 0)
        send_other(phase, source, target)

    def relay(phase, count, target):
        wait_for(relay_sem, phase, landing.at[phase, :, pl.ds(0, count), pl.ds(0, ROWS)])

        def step(core, carry):
            origin = place(my_x, my_y + 2, core)
            for number, (dx, dy) in enumerate(RELAYED):
                start_copy(
                    landing.at[phase, core * 2 + number, pl.ds(0, count), pl.ds(0, ROWS)],
                    target(origin, slot_of(origin)),
                    forward_sem.at[phase],
                    recv_sem.at[phase],
                    place(my_x + dx, my_y, my_core),
                )
            return carry

        lax.fori_loop(0, 2, step, 0)

    def wait_for(sem, phase, ref):
        pltpu.make_async_copy(ref, ref, sem.at[phase]).wait()

    some = pl.ds(0, ROWS)
    most = pl.ds(0, SPEC - 1)

    def to_base(origin, slot):
        return r1.at[origin, pl.ds(0, 1), some]

    def to_tangents(origin, slot):
        return r1.at[origin, pl.ds(1, 2), some]

    def to_flow(index):
        return lambda origin, slot: r2.at[index, slot, :, some]

    def to_slope(index):
        return lambda origin, slot: r3.at[index, origin, :, some]

    def to_evolved(origin, slot):
        return r4.at[slot, :, some]

    for parity in range(2):
        def fold(half_parity=parity):
            for index, ref in ((0, tang_ref.at[0, 0]), (1, tang_ref.at[0, 1]), (2, base_ref.at[0]), (3, base_ref.at[0])):
                lo, hi = ref[:, :HALF], ref[:, HALF:]
                value = lo + hi if half_parity == 0 else lo - hi
                folded[index * SLAB : (index + 1) * SLAB, :] = value.astype(BF16)

        fold()

        def spectrum_rows(step, carry, parity=parity):
            rows = pl.ds(pl.multiple_of(step * 192, 192), 192)
            out = lax.dot_general(
                tf_ref[parity, rows, :], folded[...], (((1,), (1,)), ((), ())), preferred_element_type=F32
            ).reshape(4, 2, PAD, 2 * LANES)
            slots = pl.ds(parity * 16 + step * 4, 4)
            s1[slots, 0] = jnp.where(low[None], out[:, 0, :, LANES:], out[:, 1, :, LANES:])
            s1[slots, 1] = out[:, 0, :, :LANES]
            s1[slots, 2] = out[:, 1, :, :LANES]
            return carry

        lax.fori_loop(0, 4, spectrum_rows, 0)

    pl.semaphore_wait(barrier, SPEC - 1 + TM - 1)
    send_all(0, lambda peer, slot: s1.at[slot, pl.ds(0, 1), some], to_base)
    send_all(1, lambda peer, slot: s1.at[slot, pl.ds(1, 2), some], to_tangents)
    r1[me] = s1[my_slot]

    lane = lax.broadcasted_iota(jnp.int32, (PAD, LANES), 1)
    row = lax.broadcasted_iota(jnp.int32, (PAD, LANES), 0)
    second = 2 * (ROWS * (me // 2) + row) + lax.rem(me, 2)
    second_keep = (second <= BAND) & (row < ROWS)
    second_wave = second.astype(F32)
    low_rows = lane < SLAB
    column = jnp.where(second == 0, 1.0, 2.0)
    to_field = column * (1.0 / float(NG * NG))
    gram_weight = jnp.where(second_keep, column * (1.0 / float(NG) ** 4), 0.0)

    def multipliers(k1, carry):
        first = k1 + 32 * lax.rem(lane, SLAB)
        first = jnp.where(first < HALF, first, first - NG)
        first_wave = first.astype(F32)
        keep = jnp.where(second_keep & (jnp.abs(first) <= BAND), 1.0, 0.0)
        square = first_wave * first_wave + second_wave * second_wave
        inverse = jnp.where(square > 0.0, 1.0 / jnp.maximum(square, 1.0), 0.0)
        decay = keep * jnp.exp(-(visc_scale / BAND**2) * time_step * square)
        mult_flow[k1] = keep * to_field * inverse * jnp.where(low_rows, -second_wave, first_wave)
        mult_decay[k1] = decay
        mult_slope[k1] = (time_step * decay) * jnp.where(
            low_rows,
            first_wave * first_wave - second_wave * second_wave,
            2.0 * first_wave * second_wave,
        )
        return carry

    lax.fori_loop(0, 32, multipliers, 0)

    def first_forward(load, target):
        def body(step, carry):
            rows = pl.ds(pl.multiple_of(step * 8, 8), 8)
            pairs = [load(i, rows) for i in range(SPEC)]
            re, im = short_transform([p[0] for p in pairs], [p[1] for p in pairs], -1.0)
            for k1 in range(32):
                c, s = twist_ref[0, k1 : k1 + 1, :], twist_ref[1, k1 : k1 + 1, :]
                target[k1, rows, :LANES] = re[k1] * c + im[k1] * s
                target[k1, rows, LANES:] = im[k1] * c - re[k1] * s
            return carry

        lax.fori_loop(0, PAD // 8, body, 0)

    def first_inverse(target):
        def body(step, carry):
            rows = pl.ds(pl.multiple_of(step * 8, 8), 8)
            res, ims = [], []
            for k1 in range(32):
                c, s = twist_ref[0, k1 : k1 + 1, :], twist_ref[1, k1 : k1 + 1, :]
                re, im = tw[k1, rows, :LANES], tw[k1, rows, LANES:]
                res.append(re * c - im * s)
                ims.append(im * c + re * s)
            re, im = short_transform(res, ims, 1.0)
            for i in range(SPEC):
                target[i, 0, rows, :] = re[i]
                target[i, 1, rows, :] = im[i]
            return carry

        lax.fori_loop(0, PAD // 8, body, 0)

    def chunks(body):
        def step(c, carry):
            body(pl.ds(c * 8, 8))
            return carry

        lax.fori_loop(0, 4, step, 0)

    def flow(source, which, index):
        def body(part):
            spectrum = dot(source[part].reshape(192, 256).astype(BF16), lane_ref[which])
            factor = mult_flow[part].reshape(192, LANES)
            scaled = jnp.concatenate([spectrum[:, :LANES] * factor, spectrum[:, LANES:] * factor], axis=1)
            tw[part] = dot(scaled.astype(BF16), lane_ref[3]).reshape(8, PAD, 256)

        chunks(body)
        first_inverse(s2.at[index])
        send_all(2 + index, lambda peer, slot: s2.at[index, peer, :, some], to_flow(index))
        r2[index, my_slot] = s2[index, me]

    sign = jnp.where(low, 1.0, -1.0)

    def load_base(i, rows):
        value = r1[i, 0, rows, :]
        return value, pltpu.roll(value, SLAB, 1) * sign

    wait_for(recv_sem, 0, r1.at[most, pl.ds(0, 1), some])
    first_forward(load_base, tb)
    flow(tb, 0, 0)
    wait_for(recv_sem, 1, r1.at[most, pl.ds(1, 2), some])
    first_forward(lambda i, rows: (r1[i, 1, rows, :], r1[i, 2, rows, :]), tt)
    flow(tt, 0, 1)
    flow(tt, 1, 2)

    def start_spectrum(part):
        spectrum = dot(tt[part].reshape(192, 256).astype(BF16), lane_ref[2])
        decay = mult_decay[part]
        zr[part] = spectrum[:, :LANES].reshape(8, PAD, LANES) * decay
        zi[part] = spectrum[:, LANES:].reshape(8, PAD, LANES) * decay

    chunks(start_spectrum)

    def second_inverse(ref, body):
        even = ref[pl.ds(0, 16)].reshape(SIDE, LANES).astype(BF16)
        odd = ref[pl.ds(16, 16)].reshape(SIDE, LANES).astype(BF16)

        def step(c, carry):
            rows = pl.ds(pl.multiple_of(c * 256, 256), 256)
            e = dot(ti_ref[0, rows, :], even)
            o = dot(ti_ref[1, rows, :], odd)
            body(c, e + o, e - o)
            return carry

        lax.fori_loop(0, 4, step, 0)

    wait_for(recv_sem, 2, r2.at[0, most, :, some])

    def keep_base(c, lower, upper):
        base_flow[pl.ds(pl.multiple_of(c * 256, 256), 256), :] = lower
        base_flow[pl.ds(pl.multiple_of(c * 256 + HALF, 256), 256), :] = upper

    second_inverse(r2.at[0], keep_base)

    def products(b, t):
        straight = b * t
        crossed = b * pltpu.roll(t, SLAB, 1)
        near = jnp.where(low, crossed, straight)
        far = pltpu.roll(jnp.where(low, straight, crossed), SLAB, 1)
        return near + far * sign

    for index in range(2):
        wait_for(recv_sem, 3 + index, r2.at[1 + index, most, :, some])

        def multiply(c, lower, upper):
            rows = pl.ds(pl.multiple_of(c * 256, 256), 256)
            lo = products(base_flow[rows, :], lower)
            hi = products(base_flow[pl.ds(pl.multiple_of(c * 256 + HALF, 256), 256), :], upper)
            product[0, rows, :] = (lo + hi).astype(BF16)
            product[1, rows, :] = (lo - hi).astype(BF16)

        second_inverse(r2.at[1 + index], multiply)

        for parity in range(2):
            def product_rows(step, carry, parity=parity, index=index):
                rows = pl.ds(pl.multiple_of(step * 192, 192), 192)
                out = dot(tf_ref[parity, rows, :], product[parity])
                s3[index, pl.ds(parity * 16 + step * 4, 4)] = out.reshape(4, 2, PAD, LANES)
                return carry

            lax.fori_loop(0, 4, product_rows, 0)

        send_all(
            5 + index,
            lambda peer, slot, index=index: s3.at[index, slot, :, some],
            to_slope(index),
        )
        r3[index, me] = s3[index, my_slot]

    for index in range(2):
        wait_for(recv_sem, 5 + index, r3.at[index, most, :, some])
        first_forward(lambda i, rows, index=index: (r3[index, i, 0, rows, :], r3[index, i, 1, rows, :]), tb)

        def add_slope(part, index=index):
            spectrum = dot(tb[part].reshape(192, 256).astype(BF16), lane_ref[2])
            factor = mult_slope[part].reshape(192, LANES)
            for half, ref in ((0, zr), (1, zi)):
                terms = spectrum[:, half * LANES : (half + 1) * LANES] * factor
                slope = terms + pltpu.roll(terms, SLAB, 1)
                slope = jnp.where(low, slope, 0.0) if index == 0 else jnp.where(low, 0.0, slope)
                ref[part] = ref[part] + slope.reshape(8, PAD, LANES)

        chunks(add_slope)

    def inner(k1, carry):
        squares, crosses = carry
        re, im = zr[k1], zi[k1]
        squares = squares + (re * re + im * im) * gram_weight
        crosses = crosses + (re * pltpu.roll(re, SLAB, 1) + im * pltpu.roll(im, SLAB, 1)) * gram_weight
        return squares, crosses

    nothing = jnp.zeros((PAD, LANES), F32)
    squares, crosses = lax.fori_loop(0, 32, inner, (nothing, nothing))

    def total(x):
        return jnp.sum(jnp.sum(x, axis=0, keepdims=True), axis=1, keepdims=True)

    lane8 = lax.broadcasted_iota(jnp.int32, (8, LANES), 1)

    def spread(first, second, third):
        return jnp.where(lane8 == 0, first, jnp.where(lane8 == 1, second, jnp.where(lane8 == 2, third, 0.0)))

    g00 = total(jnp.where(low_rows, squares, 0.0))
    g11 = total(jnp.where(low_rows, 0.0, squares))
    g01 = total(jnp.where(low_rows, crosses, 0.0))
    gs[...] = spread(g00, g01, g11)

    def share_gram(d, carry):
        start_copy(gs, gr.at[me], send_sem.at[8], recv_sem.at[8], lax.rem(me + d, SPEC))
        return carry

    lax.fori_loop(1, SPEC, share_gram, 0)
    gr[me] = gs[...]

    def final_chunk(part):
        scale = jnp.broadcast_to(to_field[None], (8, PAD, LANES))
        scaled = jnp.concatenate(
            [(zr[part] * scale).reshape(192, LANES), (zi[part] * scale).reshape(192, LANES)], axis=1
        )
        tw[part] = dot(scaled.astype(BF16), lane_ref[3]).reshape(8, PAD, 256)

    chunks(final_chunk)
    first_inverse(s4)
    send_all(7, lambda peer, slot: s4.at[peer, :, some], to_evolved)
    r4[my_slot] = s4[me]


    def pick(values, index):
        return jnp.sum(jnp.where(lane8[:1] == index, values, 0.0), axis=1, keepdims=True)

    wait_for(recv_sem, 8, gr.at[most])
    gram = jnp.sum(gr[...], axis=0)[:1]
    g00, g01, g11 = pick(gram, 0), pick(gram, 1), pick(gram, 2)
    u00 = jnp.sqrt(g00)
    u01 = g01 / u00
    u11 = jnp.sqrt(g11 - u01 * u01)
    i00, i11 = 1.0 / u00, 1.0 / u11
    i01 = -(i00 * u01) / u11
    i10 = jnp.zeros_like(i00)
    ts[...] = spread(i00, i01, i11)

    def share(d, carry):
        pltpu.make_async_remote_copy(
            src_ref=ts,
            dst_ref=tr.at[seg],
            send_sem=send_sem.at[9],
            recv_sem=recv_sem.at[9],
            device_id={"tm": lax.rem(seg + d, TM)},
            device_id_type=MESH,
        ).start()
        return carry

    lax.fori_loop(1, TM, share, 0)
    tr[seg] = ts[...]
    wait_for(recv_sem, 9, tr.at[pl.ds(0, TM - 1)])
    one, zero = jnp.ones_like(i00), jnp.zeros_like(i00)
    end00, end01, end11 = end_ref[0, 0], end_ref[0, 1], end_ref[1, 1]
    p00, p01, p10, p11 = one, zero, zero, one
    for later in range(TM - 1, -1, -1):
        values = tr[later][:1]
        active = later >= seg
        a00 = jnp.where(active, pick(values, 0), one)
        a01 = jnp.where(active, pick(values, 1), zero)
        a11 = jnp.where(active, pick(values, 2), one)
        a10 = zero
        p00, p01, p10, p11 = (
            a00 * p00 + a01 * p10,
            a00 * p01 + a01 * p11,
            a10 * p00 + a11 * p10,
            a10 * p01 + a11 * p11,
        )
    q00, q01 = p00 * end00, p00 * end01 + p01 * end11
    q10, q11 = p10 * end00, p10 * end01 + p11 * end11
    norm0 = jnp.sqrt(q00 * q00 + q10 * q10)
    norm1 = jnp.sqrt(q01 * q01 + q11 * q11)
    c00, c10, c01, c11 = q00 / norm0, q10 / norm0, q01 / norm1, q11 / norm1
    small = jnp.zeros((8, LANES), F32)
    for number, value in enumerate((c00, c01, c10, c11, i00, i01, i10, i11, jnp.log(u00), jnp.log(u11))):
        small = jnp.where(lane8 == number, value, small)
    small_ref[...] = small

    wait_for(recv_sem, 7, r4.at[most, :, some])
    even_ref[...] = r4[pl.ds(0, 16)].reshape(SIDE, LANES).T.astype(BF16)
    odd_ref[...] = r4[pl.ds(16, 16)].reshape(SIDE, LANES).T.astype(BF16)

    wait_for(send_sem, 0, s1.at[most, pl.ds(0, 1), some])
    wait_for(send_sem, 1, s1.at[most, pl.ds(1, 2), some])
    for index in range(3):
        wait_for(send_sem, 2 + index, s2.at[index, most, :, some])
    for index in range(2):
        wait_for(send_sem, 5 + index, s3.at[index, most, :, some])
    wait_for(send_sem, 7, s4.at[most, :, some])
    wait_for(send_sem, 8, gr.at[most])
    wait_for(send_sem, 9, tr.at[pl.ds(0, TM - 1)])


def finish(even_ref, odd_ref, small_ref, tf_ref, tang_ref, cov_ref, basis_ref, coef_ref, growth_ref, upper):
    step = pl.program_id(0)
    small = small_ref[:1, :]
    lane = lax.broadcasted_iota(jnp.int32, (1, LANES), 1)

    def pick(index):
        return jnp.sum(jnp.where(lane == index, small, 0.0), axis=1, keepdims=True)

    c00, c01, c10, c11, i00, i01, i10, i11, log0, log1 = [pick(number) for number in range(10)]

    def write(value):
        first, second = value[:SLAB], value[SLAB:]
        basis_ref[0, 0] = first * i00 + second * i10
        basis_ref[0, 1] = first * i01 + second * i11

    @pl.when(step < 2)
    def _():
        e = dot(even_ref[...], tf_ref[0])
        o = dot(odd_ref[...], tf_ref[1])
        upper[step] = e - o
        write(e + o)

    @pl.when(step >= 2)
    def _():
        write(upper[step - 2])

    cov_ref[0, 0] = tang_ref[0, 0] * c00 + tang_ref[0, 1] * c10
    cov_ref[0, 1] = tang_ref[0, 0] * c01 + tang_ref[0, 1] * c11
    across = lax.broadcasted_iota(jnp.int32, (2, 2), 1)
    down = lax.broadcasted_iota(jnp.int32, (2, 2), 0)
    coef_ref[0] = jnp.where(
        down == 0, jnp.where(across == 0, c00, c01), jnp.where(across == 0, c10, c11)
    )
    pair = lax.broadcasted_iota(jnp.int32, (1, 2), 1)
    growth_ref[...] = jnp.where(pair == 0, log0, log1)


def shards(base_flow, tangents, end_matrix):
    rows = row_tables()
    tf = jnp.asarray(rows.astype(ml_dtypes.bfloat16))
    ti = jnp.asarray(np.ascontiguousarray(rows.transpose(0, 2, 1)).astype(ml_dtypes.bfloat16))
    lanes = jnp.asarray(lane_tables().astype(ml_dtypes.bfloat16))
    twist = jnp.asarray(twist_tables().astype(np.float32))
    vmem = pl.BlockSpec(memory_space=pltpu.VMEM)
    smem = pl.BlockSpec(memory_space=pltpu.SMEM)

    def buffer(*lead):
        return pltpu.VMEM(lead + (PAD, LANES), F32)

    even, odd, small = pl.pallas_call(
        kernel,
        out_shape=(
            jax.ShapeDtypeStruct((LANES, SIDE), BF16),
            jax.ShapeDtypeStruct((LANES, SIDE), BF16),
            jax.ShapeDtypeStruct((8, LANES), F32),
        ),
        in_specs=[vmem, vmem, smem, vmem, vmem, vmem, vmem],
        out_specs=(vmem, vmem, vmem),
        scratch_shapes=[
            buffer(SPEC, 3),
            buffer(SPEC, 3),
            buffer(3, SPEC, 2),
            buffer(3, SPEC, 2),
            buffer(2, SPEC, 2),
            buffer(2, SPEC, 2),
            buffer(SPEC, 2),
            buffer(SPEC, 2),
            pltpu.VMEM((8, LANES), F32),
            pltpu.VMEM((SPEC, 8, LANES), F32),
            pltpu.VMEM((8, LANES), F32),
            pltpu.VMEM((TM, 8, LANES), F32),
            pltpu.VMEM((32, PAD, 256), F32),
            pltpu.VMEM((32, PAD, 256), F32),
            pltpu.VMEM((32, PAD, 256), F32),
            pltpu.VMEM((4 * SLAB, HALF), BF16),
            buffer(32),
            buffer(32),
            buffer(32),
            buffer(32),
            buffer(32),
            pltpu.VMEM((NG, LANES), F32),
            pltpu.VMEM((2, HALF, LANES), BF16),
            buffer(8, 4, 2),
            pltpu.SemaphoreType.DMA((8,)),
            pltpu.SemaphoreType.DMA((8,)),
            pltpu.SemaphoreType.DMA((10,)),
            pltpu.SemaphoreType.DMA((10,)),
        ],
        compiler_params=pltpu.CompilerParams(
            collective_id=0, has_side_effects=True, vmem_limit_bytes=56 * 1024 * 1024
        ),
        cost_estimate=pl.CostEstimate(flops=12_000_000_000, bytes_accessed=12_000_000, transcendentals=0),
    )(base_flow, tangents, end_matrix, tf, ti, lanes, twist)

    whole = lambda *shape: pl.BlockSpec(shape, lambda g: (0,) * len(shape))
    wide = pl.BlockSpec((1, K, SLAB, 512), lambda g: (0, 0, 0, g))
    return pl.pallas_call(
        finish,
        grid=(4,),
        out_shape=(
            jax.ShapeDtypeStruct((1, K, SLAB, NG), F32),
            jax.ShapeDtypeStruct((1, K, SLAB, NG), F32),
            jax.ShapeDtypeStruct((1, K, K), F32),
            jax.ShapeDtypeStruct((1, K), F32),
        ),
        in_specs=[
            whole(LANES, SIDE),
            whole(LANES, SIDE),
            whole(8, LANES),
            pl.BlockSpec((2, SIDE, 512), lambda g: (0, 0, jnp.minimum(g, 1))),
            wide,
        ],
        out_specs=(wide, wide, whole(1, K, K), whole(1, K)),
        scratch_shapes=[pltpu.VMEM((2, LANES, 512), F32)],
        compiler_params=pltpu.CompilerParams(vmem_limit_bytes=24 * 1024 * 1024),
        cost_estimate=pl.CostEstimate(flops=400_000_000, bytes_accessed=6_500_000, transcendentals=0),
    )(even, odd, small, tf, tangents)


def solution(mesh):
    in_specs = (P("tm", "spec", None), P("tm", None, "spec", None), P())
    out_specs = (
        P("tm", None, "spec", None),
        P("tm", None, "spec", None),
        P("tm", None, None),
        P("tm", None),
    )
    return jax.shard_map(shards, mesh=mesh, in_specs=in_specs, out_specs=out_specs, check_vma=False)
```

```python
import functools
import math

import jax
import jax.numpy as jnp
import ml_dtypes
import numpy as np
from jax import lax
from jax.experimental import pallas as pl
from jax.experimental.pallas import tpu as pltpu
from jax.sharding import PartitionSpec as P

NG = 2048
HALF = NG // 2
K = 2
SPEC = 32
TM = 8
SLAB = NG // SPEC
BAND = NG // 3
ROWS = 22
PAD = 24
LANES = 128
SIDE = 16 * 2 * PAD

DIRECT = ((2, 2), (1, 2), (2, 1), (3, 2), (2, 3), (2, 0), (0, 2), (1, 1), (3, 3), (1, 3), (3, 1), (1, 0), (0, 1), (3, 0), (0, 3))

time_step = 0.1
visc_scale = 15.0
MESH = pl.DeviceIdType.MESH
F32 = jnp.float32
BF16 = jnp.bfloat16


def row_tables():
    owner = np.arange(16)[:, None, None]
    part = np.arange(2)[None, :, None]
    row = np.arange(PAD)[None, None, :]
    y = np.arange(HALF)[None, :]
    tables = []
    for parity in range(2):
        wave = 2 * (ROWS * owner + row) + parity
        valid = np.broadcast_to((wave <= BAND) & (row < ROWS), (16, 2, PAD)).reshape(SIDE, 1)
        waves = np.broadcast_to(wave, (16, 2, PAD)).reshape(SIDE, 1)
        parts = np.broadcast_to(part, (16, 2, PAD)).reshape(SIDE, 1)
        angle = (waves * y % NG) * (2.0 * math.pi / NG)
        tables.append(np.where(valid, np.where(parts == 0, np.cos(angle), -np.sin(angle)), 0.0))
    return np.stack(tables)


def lane_tables():
    index = np.arange(SLAB)
    angle = (index[:, None] * index[None, :] % SLAB) * (2.0 * math.pi / SLAB)
    cos, sin, zero = np.cos(angle), np.sin(angle), np.zeros((SLAB, SLAB))
    pair_forward = np.block(
        [[cos, zero, -sin, zero], [zero, cos, zero, -sin], [sin, zero, cos, zero], [zero, sin, zero, cos]]
    )
    pair_inverse = np.block(
        [[cos, zero, sin, zero], [zero, cos, zero, sin], [-sin, zero, cos, zero], [zero, -sin, zero, cos]]
    )
    twice = []
    for half in range(2):
        real = pair_forward[:, half * SLAB : (half + 1) * SLAB]
        imag = pair_forward[:, (2 + half) * SLAB : (3 + half) * SLAB]
        twice.append(np.concatenate([imag, imag, -real, -real], axis=1))
    return np.stack([twice[0], twice[1], pair_forward, pair_inverse])


def twist_tables():
    first = np.arange(32)[:, None]
    place = (np.arange(LANES) % SLAB)[None, :]
    angle = (first * place) * (2.0 * math.pi / NG)
    return np.stack([np.cos(angle), np.sin(angle)])


def turned(re, im, angle):
    c, s = math.cos(angle), math.sin(angle)
    if abs(s) < 1e-9 and c > 0:
        return re, im
    if abs(c) < 1e-9:
        return (-im, re) if s > 0 else (im, -re)
    if abs(abs(c) - abs(s)) < 1e-9:
        root = math.sqrt(0.5)
        sc, ss = (root if c > 0 else -root), (root if s > 0 else -root)
        if sc == ss:
            return (re - im) * sc, (re + im) * sc
        return (re + im) * sc, (im - re) * sc
    return re * c - im * s, re * s + im * c


def short_transform(res, ims, sign):
    count = len(res)
    if count == 1:
        return res, ims
    er, ei = short_transform(res[0::2], ims[0::2], sign)
    dr, di = short_transform(res[1::2], ims[1::2], sign)
    half = count // 2
    out_r, out_i = [None] * count, [None] * count
    for k in range(half):
        tr, ti = turned(dr[k], di[k], sign * 2.0 * math.pi * k / count)
        out_r[k], out_i[k] = er[k] + tr, ei[k] + ti
        out_r[k + half], out_i[k + half] = er[k] - tr, ei[k] - ti
    return out_r, out_i


def dot(a, b):
    return jnp.dot(a, b, preferred_element_type=F32)


def kernel(
    base_ref,
    tang_ref,
    end_ref,
    tf_hbm,
    ti_hbm,
    lane_ref,
    twist_ref,
    even_ref,
    odd_ref,
    small_ref,
    s1,
    r1,
    s2,
    r2,
    s3,
    r3,
    s4,
    r4,
    gs,
    gr,
    ts,
    tr,
    tb,
    tt,
    tw,
    folded,
    zr,
    zi,
    mult_flow,
    mult_slope,
    mult_decay,
    base_flow,
    product,
    tf_ref,
    ti_ref,
    load_sem,
    send_sem,
    recv_sem,
):
    me = lax.axis_index("spec")
    my_x, my_y, my_core = me // 8, lax.rem(me // 2, 4), lax.rem(me, 2)
    seg = lax.axis_index("tm")
    my_slot = lax.rem(me, 2) * 16 + me // 2
    low = lax.broadcasted_iota(jnp.int32, (1, LANES), 1) < SLAB

    loads = [
        pltpu.make_async_copy(source.at[parity], target.at[parity], load_sem.at[number * 2 + parity])
        for number, (source, target) in enumerate(((tf_hbm, tf_ref), (ti_hbm, ti_ref)))
        for parity in range(2)
    ]
    for load in loads:
        load.start()

    barrier = pltpu.get_barrier_semaphore()

    def greet(d, carry):
        pl.semaphore_signal(barrier, inc=1, device_id={"spec": lax.rem(me + d, SPEC)}, device_id_type=MESH)
        return carry

    for ref in (r1, r2, r3, r4):
        lead = ref.shape[:-2]
        ref[(slice(None),) * len(lead) + (slice(16, 24), slice(None))] = jnp.zeros(lead + (8, LANES), F32)

    lax.fori_loop(1, SPEC, greet, 0)

    def greet_segment(d, carry):
        pl.semaphore_signal(barrier, inc=1, device_id={"tm": lax.rem(seg + d, TM)}, device_id_type=MESH)
        return carry

    lax.fori_loop(1, TM, greet_segment, 0)

    def place(x, y, core):
        return (lax.rem(x, 4) * 4 + lax.rem(y, 4)) * 2 + core

    def slot_of(device):
        return lax.rem(device, 2) * 16 + device // 2

    def start_copy(source, target, out_sem, in_sem, device):
        pltpu.make_async_remote_copy(
            src_ref=source,
            dst_ref=target,
            send_sem=out_sem,
            recv_sem=in_sem,
            device_id={"spec": device},
            device_id_type=MESH,
        ).start()

    def send_core(phase, core, source, target):
        for dx, dy in DIRECT:
            peer = place(my_x + dx, my_y + dy, core)
            start_copy(
                source(peer, slot_of(peer)), target(me, my_slot), send_sem.at[phase], recv_sem.at[phase], peer
            )

    def send_other(phase, source, target):
        peer = place(my_x, my_y, 1 - my_core)
        start_copy(
            source(peer, slot_of(peer)), target(me, my_slot), send_sem.at[phase], recv_sem.at[phase], peer
        )

    def send_all(phase, source, target):
        def step(core, carry):
            send_core(phase, core, source, target)
            return carry

        lax.fori_loop(0, 2, step, 0)
        send_other(phase, source, target)

    def wait_for(sem, phase, ref):
        pltpu.make_async_copy(ref, ref, sem.at[phase]).wait()

    some = pl.ds(0, ROWS)
    front = pl.ds(0, 16)
    back = pl.ds(16, ROWS - 16)
    most = pl.ds(0, SPEC - 1)

    def to_base(origin, slot):
        return r1.at[origin, pl.ds(0, 1), some]

    def to_tangents(origin, slot):
        return r1.at[origin, pl.ds(1, 2), some]

    def to_flow(index):
        return lambda origin, slot: r2.at[index, slot, :, some]

    def to_slope(index, rows):
        return lambda origin, slot: r3.at[index, origin, :, rows]

    def to_evolved(rows):
        return lambda origin, slot: r4.at[slot, :, rows]

    for parity in range(2):
        def fold(half_parity=parity):
            for index, ref in ((0, tang_ref.at[0, 0]), (1, tang_ref.at[0, 1]), (2, base_ref.at[0]), (3, base_ref.at[0])):
                lo, hi = ref[:, :HALF], ref[:, HALF:]
                value = lo + hi if half_parity == 0 else lo - hi
                folded[index * SLAB : (index + 1) * SLAB, :] = value.astype(BF16)

        fold()
        loads[parity].wait()

        def spectrum_rows(step, carry, parity=parity):
            rows = pl.ds(pl.multiple_of(step * 192, 192), 192)
            out = lax.dot_general(
                tf_ref[parity, rows, :], folded[...], (((1,), (1,)), ((), ())), preferred_element_type=F32
            ).reshape(4, 2, PAD, 2 * LANES)
            slots = pl.ds(parity * 16 + step * 4, 4)
            s1[slots, 0] = jnp.where(low[None], out[:, 0, :, LANES:], out[:, 1, :, LANES:])
            s1[slots, 1] = out[:, 0, :, :LANES]
            s1[slots, 2] = out[:, 1, :, :LANES]
            return carry

        lax.fori_loop(0, 4, spectrum_rows, 0)

    pl.semaphore_wait(barrier, SPEC - 1 + TM - 1)
    send_all(0, lambda peer, slot: s1.at[slot, pl.ds(0, 1), some], to_base)
    send_all(1, lambda peer, slot: s1.at[slot, pl.ds(1, 2), some], to_tangents)
    r1[me] = s1[my_slot]

    lane = lax.broadcasted_iota(jnp.int32, (PAD, LANES), 1)
    row = lax.broadcasted_iota(jnp.int32, (PAD, LANES), 0)
    second = 2 * (ROWS * (me // 2) + row) + lax.rem(me, 2)
    second_keep = (second <= BAND) & (row < ROWS)
    second_wave = second.astype(F32)
    low_rows = lane < SLAB
    column = jnp.where(second == 0, 1.0, 2.0)
    to_field = column * (1.0 / float(NG * NG))
    gram_weight = jnp.where(second_keep, column * (1.0 / float(NG) ** 4), 0.0)

    def multipliers(k1, carry):
        first = k1 + 32 * lax.rem(lane, SLAB)
        first = jnp.where(first < HALF, first, first - NG)
        first_wave = first.astype(F32)
        keep = jnp.where(second_keep & (jnp.abs(first) <= BAND), 1.0, 0.0)
        square = first_wave * first_wave + second_wave * second_wave
        inverse = jnp.where(square > 0.0, 1.0 / jnp.maximum(square, 1.0), 0.0)
        decay = keep * jnp.exp(-(visc_scale / BAND**2) * time_step * square)
        mult_flow[k1] = keep * to_field * inverse * jnp.where(low_rows, -second_wave, first_wave)
        mult_decay[k1] = decay
        mult_slope[k1] = (time_step * decay) * jnp.where(
            low_rows,
            first_wave * first_wave - second_wave * second_wave,
            2.0 * first_wave * second_wave,
        )
        return carry

    lax.fori_loop(0, 32, multipliers, 0)

    def first_forward(load, target, start=0, stop=PAD // 8):
        def body(step, carry):
            rows = pl.ds(pl.multiple_of(step * 8, 8), 8)
            pairs = [load(i, rows) for i in range(SPEC)]
            re, im = short_transform([p[0] for p in pairs], [p[1] for p in pairs], -1.0)
            for k1 in range(32):
                c, s = twist_ref[0, k1 : k1 + 1, :], twist_ref[1, k1 : k1 + 1, :]
                target[k1, rows, :LANES] = re[k1] * c + im[k1] * s
                target[k1, rows, LANES:] = im[k1] * c - re[k1] * s
            return carry

        lax.fori_loop(start, stop, body, 0)

    def first_inverse(target, start=0, stop=PAD // 8):
        def body(step, carry):
            rows = pl.ds(pl.multiple_of(step * 8, 8), 8)
            res, ims = [], []
            for k1 in range(32):
                c, s = twist_ref[0, k1 : k1 + 1, :], twist_ref[1, k1 : k1 + 1, :]
                re, im = tw[k1, rows, :LANES], tw[k1, rows, LANES:]
                res.append(re * c - im * s)
                ims.append(im * c + re * s)
            re, im = short_transform(res, ims, 1.0)
            for i in range(SPEC):
                target[i, 0, rows, :] = re[i]
                target[i, 1, rows, :] = im[i]
            return carry

        lax.fori_loop(start, stop, body, 0)

    def chunks(body):
        def step(c, carry):
            body(pl.ds(c * 8, 8))
            return carry

        lax.fori_loop(0, 4, step, 0)

    def flow(source, which, index):
        def body(part):
            spectrum = dot(source[part].reshape(192, 256).astype(BF16), lane_ref[which])
            factor = mult_flow[part].reshape(192, LANES)
            scaled = jnp.concatenate([spectrum[:, :LANES] * factor, spectrum[:, LANES:] * factor], axis=1)
            tw[part] = dot(scaled.astype(BF16), lane_ref[3]).reshape(8, PAD, 256)

        chunks(body)
        first_inverse(s2.at[index])
        send_all(2 + index, lambda peer, slot: s2.at[index, peer, :, some], to_flow(index))
        r2[index, my_slot] = s2[index, me]

    sign = jnp.where(low, 1.0, -1.0)

    def load_base(i, rows):
        value = r1[i, 0, rows, :]
        return value, pltpu.roll(value, SLAB, 1) * sign

    wait_for(recv_sem, 0, r1.at[most, pl.ds(0, 1), some])
    first_forward(load_base, tb)
    flow(tb, 0, 0)
    wait_for(recv_sem, 1, r1.at[most, pl.ds(1, 2), some])
    first_forward(lambda i, rows: (r1[i, 1, rows, :], r1[i, 2, rows, :]), tt)
    flow(tt, 0, 1)
    flow(tt, 1, 2)

    def start_spectrum(part):
        spectrum = dot(tt[part].reshape(192, 256).astype(BF16), lane_ref[2])
        decay = mult_decay[part]
        zr[part] = spectrum[:, :LANES].reshape(8, PAD, LANES) * decay
        zi[part] = spectrum[:, LANES:].reshape(8, PAD, LANES) * decay

    chunks(start_spectrum)

    def second_inverse(ref, body):
        even = ref[pl.ds(0, 16)].reshape(SIDE, LANES).astype(BF16)
        odd = ref[pl.ds(16, 16)].reshape(SIDE, LANES).astype(BF16)

        def step(c, carry):
            rows = pl.ds(pl.multiple_of(c * 256, 256), 256)
            e = dot(ti_ref[0, rows, :], even)
            o = dot(ti_ref[1, rows, :], odd)
            body(c, e + o, e - o)
            return carry

        lax.fori_loop(0, 4, step, 0)

    loads[2].wait()
    loads[3].wait()
    wait_for(recv_sem, 2, r2.at[0, most, :, some])

    def keep_base(c, lower, upper):
        base_flow[pl.ds(pl.multiple_of(c * 256, 256), 256), :] = lower
        base_flow[pl.ds(pl.multiple_of(c * 256 + HALF, 256), 256), :] = upper

    second_inverse(r2.at[0], keep_base)

    def products(b, t):
        straight = b * t
        crossed = b * pltpu.roll(t, SLAB, 1)
        near = jnp.where(low, crossed, straight)
        far = pltpu.roll(jnp.where(low, straight, crossed), SLAB, 1)
        return near + far * sign

    for index in range(2):
        wait_for(recv_sem, 3 + index, r2.at[1 + index, most, :, some])

        def multiply(c, lower, upper):
            rows = pl.ds(pl.multiple_of(c * 256, 256), 256)
            lo = products(base_flow[rows, :], lower)
            hi = products(base_flow[pl.ds(pl.multiple_of(c * 256 + HALF, 256), 256), :], upper)
            product[0, rows, :] = (lo + hi).astype(BF16)
            product[1, rows, :] = (lo - hi).astype(BF16)

        second_inverse(r2.at[1 + index], multiply)

        for parity in range(2):
            def product_rows(step, carry, parity=parity, index=index):
                rows = pl.ds(pl.multiple_of(step * 192, 192), 192)
                out = dot(tf_ref[parity, rows, :], product[parity])
                s3[index, pl.ds(parity * 16 + step * 4, 4)] = out.reshape(4, 2, PAD, LANES)
                return carry

            lax.fori_loop(0, 4, product_rows, 0)

        if index == 0:
            send_all(5, lambda peer, slot: s3.at[0, slot, :, some], to_slope(0, some))
        else:
            send_all(6, lambda peer, slot: s3.at[1, slot, :, front], to_slope(1, front))
            send_all(10, lambda peer, slot: s3.at[1, slot, :, back], to_slope(1, back))
        r3[index, me] = s3[index, my_slot]

    def slope(index, start, count):
        rows = pl.ds(start, count)
        first_forward(
            lambda i, rows: (r3[index, i, 0, rows, :], r3[index, i, 1, rows, :]),
            tb,
            start // 8,
            (start + count) // 8,
        )

        def add_slope(part):
            spectrum = dot(tb[part, rows].reshape(8 * count, 256).astype(BF16), lane_ref[2])
            factor = mult_slope[part, rows].reshape(8 * count, LANES)
            for half, ref in ((0, zr), (1, zi)):
                terms = spectrum[:, half * LANES : (half + 1) * LANES] * factor
                both = terms + pltpu.roll(terms, SLAB, 1)
                both = jnp.where(low, both, 0.0) if index == 0 else jnp.where(low, 0.0, both)
                ref[part, rows] = ref[part, rows] + both.reshape(8, count, LANES)

        chunks(add_slope)

    def evolve(start, count):
        rows = pl.ds(start, count)

        def final_chunk(part):
            scale = jnp.broadcast_to(to_field[None, start : start + count], (8, count, LANES))
            scaled = jnp.concatenate(
                [(ref[part, rows] * scale).reshape(8 * count, LANES) for ref in (zr, zi)], axis=1
            )
            tw[part, rows] = dot(scaled.astype(BF16), lane_ref[3]).reshape(8, count, 256)

        chunks(final_chunk)
        first_inverse(s4, start // 8, (start + count) // 8)

    wait_for(recv_sem, 5, r3.at[0, most, :, some])
    slope(0, 0, PAD)
    wait_for(recv_sem, 6, r3.at[1, most, :, front])
    slope(1, 0, 16)
    evolve(0, 16)
    send_all(7, lambda peer, slot: s4.at[peer, :, front], to_evolved(front))
    wait_for(recv_sem, 10, r3.at[1, most, :, back])
    slope(1, 16, 8)

    def inner(k1, carry):
        squares, crosses = carry
        re, im = zr[k1], zi[k1]
        squares = squares + (re * re + im * im) * gram_weight
        crosses = crosses + (re * pltpu.roll(re, SLAB, 1) + im * pltpu.roll(im, SLAB, 1)) * gram_weight
        return squares, crosses

    nothing = jnp.zeros((PAD, LANES), F32)
    squares, crosses = lax.fori_loop(0, 32, inner, (nothing, nothing))

    def total(x):
        return jnp.sum(jnp.sum(x, axis=0, keepdims=True), axis=1, keepdims=True)

    lane8 = lax.broadcasted_iota(jnp.int32, (8, LANES), 1)

    def spread(first, second, third):
        return jnp.where(lane8 == 0, first, jnp.where(lane8 == 1, second, jnp.where(lane8 == 2, third, 0.0)))

    g00 = total(jnp.where(low_rows, squares, 0.0))
    g11 = total(jnp.where(low_rows, 0.0, squares))
    g01 = total(jnp.where(low_rows, crosses, 0.0))
    gs[...] = spread(g00, g01, g11)

    def share_gram(d, carry):
        start_copy(gs, gr.at[me], send_sem.at[8], recv_sem.at[8], lax.rem(me + d, SPEC))
        return carry

    lax.fori_loop(1, SPEC, share_gram, 0)
    gr[me] = gs[...]

    evolve(16, 8)
    send_all(11, lambda peer, slot: s4.at[peer, :, back], to_evolved(back))
    r4[my_slot] = s4[me]


    def pick(values, index):
        return jnp.sum(jnp.where(lane8[:1] == index, values, 0.0), axis=1, keepdims=True)

    wait_for(recv_sem, 8, gr.at[most])
    gram = jnp.sum(gr[...], axis=0)[:1]
    g00, g01, g11 = pick(gram, 0), pick(gram, 1), pick(gram, 2)
    u00 = jnp.sqrt(g00)
    u01 = g01 / u00
    u11 = jnp.sqrt(g11 - u01 * u01)
    i00, i11 = 1.0 / u00, 1.0 / u11
    i01 = -(i00 * u01) / u11
    i10 = jnp.zeros_like(i00)
    ts[...] = spread(i00, i01, i11)

    def share(d, carry):
        pltpu.make_async_remote_copy(
            src_ref=ts,
            dst_ref=tr.at[seg],
            send_sem=send_sem.at[9],
            recv_sem=recv_sem.at[9],
            device_id={"tm": lax.rem(seg + d, TM)},
            device_id_type=MESH,
        ).start()
        return carry

    lax.fori_loop(1, TM, share, 0)
    tr[seg] = ts[...]
    wait_for(recv_sem, 9, tr.at[pl.ds(0, TM - 1)])
    one, zero = jnp.ones_like(i00), jnp.zeros_like(i00)
    end00, end01, end11 = end_ref[0, 0], end_ref[0, 1], end_ref[1, 1]
    p00, p01, p10, p11 = one, zero, zero, one
    for later in range(TM - 1, -1, -1):
        values = tr[later][:1]
        active = later >= seg
        a00 = jnp.where(active, pick(values, 0), one)
        a01 = jnp.where(active, pick(values, 1), zero)
        a11 = jnp.where(active, pick(values, 2), one)
        a10 = zero
        p00, p01, p10, p11 = (
            a00 * p00 + a01 * p10,
            a00 * p01 + a01 * p11,
            a10 * p00 + a11 * p10,
            a10 * p01 + a11 * p11,
        )
    q00, q01 = p00 * end00, p00 * end01 + p01 * end11
    q10, q11 = p10 * end00, p10 * end01 + p11 * end11
    norm0 = jnp.sqrt(q00 * q00 + q10 * q10)
    norm1 = jnp.sqrt(q01 * q01 + q11 * q11)
    c00, c10, c01, c11 = q00 / norm0, q10 / norm0, q01 / norm1, q11 / norm1
    small = jnp.zeros((8, LANES), F32)
    for number, value in enumerate((c00, c01, c10, c11, i00, i01, i10, i11, jnp.log(u00), jnp.log(u11))):
        small = jnp.where(lane8 == number, value, small)
    small_ref[...] = small

    wait_for(recv_sem, 7, r4.at[most, :, front])
    wait_for(recv_sem, 11, r4.at[most, :, back])
    even_ref[...] = r4[pl.ds(0, 16)].reshape(SIDE, LANES).T.astype(BF16)
    odd_ref[...] = r4[pl.ds(16, 16)].reshape(SIDE, LANES).T.astype(BF16)

    wait_for(send_sem, 0, s1.at[most, pl.ds(0, 1), some])
    wait_for(send_sem, 1, s1.at[most, pl.ds(1, 2), some])
    for index in range(3):
        wait_for(send_sem, 2 + index, s2.at[index, most, :, some])
    wait_for(send_sem, 5, s3.at[0, most, :, some])
    wait_for(send_sem, 6, s3.at[1, most, :, front])
    wait_for(send_sem, 10, s3.at[1, most, :, back])
    wait_for(send_sem, 7, s4.at[most, :, front])
    wait_for(send_sem, 11, s4.at[most, :, back])
    wait_for(send_sem, 8, gr.at[most])
    wait_for(send_sem, 9, tr.at[pl.ds(0, TM - 1)])


def finish(even_ref, odd_ref, small_ref, tf_ref, tang_ref, cov_ref, basis_ref, coef_ref, growth_ref, upper):
    step = pl.program_id(0)
    small = small_ref[:1, :]
    lane = lax.broadcasted_iota(jnp.int32, (1, LANES), 1)

    def pick(index):
        return jnp.sum(jnp.where(lane == index, small, 0.0), axis=1, keepdims=True)

    c00, c01, c10, c11, i00, i01, i10, i11, log0, log1 = [pick(number) for number in range(10)]

    def write(value):
        first, second = value[:SLAB], value[SLAB:]
        basis_ref[0, 0] = first * i00 + second * i10
        basis_ref[0, 1] = first * i01 + second * i11

    @pl.when(step < 2)
    def _():
        e = dot(even_ref[...], tf_ref[0])
        o = dot(odd_ref[...], tf_ref[1])
        upper[step] = e - o
        write(e + o)

    @pl.when(step >= 2)
    def _():
        write(upper[step - 2])

    cov_ref[0, 0] = tang_ref[0, 0] * c00 + tang_ref[0, 1] * c10
    cov_ref[0, 1] = tang_ref[0, 0] * c01 + tang_ref[0, 1] * c11
    across = lax.broadcasted_iota(jnp.int32, (2, 2), 1)
    down = lax.broadcasted_iota(jnp.int32, (2, 2), 0)
    coef_ref[0] = jnp.where(
        down == 0, jnp.where(across == 0, c00, c01), jnp.where(across == 0, c10, c11)
    )
    pair = lax.broadcasted_iota(jnp.int32, (1, 2), 1)
    growth_ref[...] = jnp.where(pair == 0, log0, log1)


def shards(base_flow, tangents, end_matrix):
    rows = row_tables()
    tf = jnp.asarray(rows.astype(ml_dtypes.bfloat16))
    ti = jnp.asarray(np.ascontiguousarray(rows.transpose(0, 2, 1)).astype(ml_dtypes.bfloat16))
    lanes = jnp.asarray(lane_tables().astype(ml_dtypes.bfloat16))
    twist = jnp.asarray(twist_tables().astype(np.float32))
    vmem = pl.BlockSpec(memory_space=pltpu.VMEM)
    smem = pl.BlockSpec(memory_space=pltpu.SMEM)
    hbm = pl.BlockSpec(memory_space=pl.ANY)

    def buffer(*lead):
        return pltpu.VMEM(lead + (PAD, LANES), F32)

    even, odd, small = pl.pallas_call(
        kernel,
        out_shape=(
            pltpu.VMEM((LANES, SIDE), BF16),
            pltpu.VMEM((LANES, SIDE), BF16),
            pltpu.VMEM((8, LANES), F32),
        ),
        in_specs=[vmem, vmem, smem, hbm, hbm, vmem, vmem],
        out_specs=(vmem, vmem, vmem),
        scratch_shapes=[
            buffer(SPEC, 3),
            buffer(SPEC, 3),
            buffer(3, SPEC, 2),
            buffer(3, SPEC, 2),
            buffer(2, SPEC, 2),
            buffer(2, SPEC, 2),
            buffer(SPEC, 2),
            buffer(SPEC, 2),
            pltpu.VMEM((8, LANES), F32),
            pltpu.VMEM((SPEC, 8, LANES), F32),
            pltpu.VMEM((8, LANES), F32),
            pltpu.VMEM((TM, 8, LANES), F32),
            pltpu.VMEM((32, PAD, 256), F32),
            pltpu.VMEM((32, PAD, 256), F32),
            pltpu.VMEM((32, PAD, 256), F32),
            pltpu.VMEM((4 * SLAB, HALF), BF16),
            buffer(32),
            buffer(32),
            buffer(32),
            buffer(32),
            buffer(32),
            pltpu.VMEM((NG, LANES), F32),
            pltpu.VMEM((2, HALF, LANES), BF16),
            pltpu.VMEM((2, SIDE, HALF), BF16),
            pltpu.VMEM((2, HALF, SIDE), BF16),
            pltpu.SemaphoreType.DMA((4,)),
            pltpu.SemaphoreType.DMA((12,)),
            pltpu.SemaphoreType.DMA((12,)),
        ],
        compiler_params=pltpu.CompilerParams(
            collective_id=0, has_side_effects=True, vmem_limit_bytes=56 * 1024 * 1024
        ),
        cost_estimate=pl.CostEstimate(flops=12_000_000_000, bytes_accessed=12_000_000, transcendentals=0),
    )(base_flow, tangents, end_matrix, tf, ti, lanes, twist)

    whole = lambda *shape: pl.BlockSpec(shape, lambda g: (0,) * len(shape))
    wide = pl.BlockSpec((1, K, SLAB, 512), lambda g: (0, 0, 0, g))
    return pl.pallas_call(
        finish,
        grid=(4,),
        out_shape=(
            jax.ShapeDtypeStruct((1, K, SLAB, NG), F32),
            jax.ShapeDtypeStruct((1, K, SLAB, NG), F32),
            jax.ShapeDtypeStruct((1, K, K), F32),
            jax.ShapeDtypeStruct((1, K), F32),
        ),
        in_specs=[
            whole(LANES, SIDE),
            whole(LANES, SIDE),
            whole(8, LANES),
            pl.BlockSpec((2, SIDE, 512), lambda g: (0, 0, jnp.minimum(g, 1))),
            wide,
        ],
        out_specs=(wide, wide, whole(1, K, K), whole(1, K)),
        scratch_shapes=[pltpu.VMEM((2, LANES, 512), F32)],
        compiler_params=pltpu.CompilerParams(vmem_limit_bytes=24 * 1024 * 1024),
        cost_estimate=pl.CostEstimate(flops=400_000_000, bytes_accessed=6_500_000, transcendentals=0),
    )(even, odd, small, tf, tangents)


def solution(mesh):
    in_specs = (P("tm", "spec", None), P("tm", None, "spec", None), P())
    out_specs = (
        P("tm", None, "spec", None),
        P("tm", None, "spec", None),
        P("tm", None, None),
        P("tm", None),
    )
    return jax.shard_map(shards, mesh=mesh, in_specs=in_specs, out_specs=out_specs, check_vma=False)
```

```python
import functools
import math

import jax
import jax.numpy as jnp
import ml_dtypes
import numpy as np
from jax import lax
from jax.experimental import pallas as pl
from jax.experimental.pallas import tpu as pltpu
from jax.sharding import PartitionSpec as P

NG = 2048
HALF = NG // 2
K = 2
SPEC = 32
TM = 8
SLAB = NG // SPEC
BAND = NG // 3
ROWS = 22
PAD = 24
LANES = 128
SIDE = 16 * 2 * PAD

DIRECT = ((2, 2), (1, 2), (2, 1), (3, 2), (2, 3), (2, 0), (0, 2), (1, 1), (3, 3), (1, 3), (3, 1), (1, 0), (0, 1), (3, 0), (0, 3))

time_step = 0.1
visc_scale = 15.0
MESH = pl.DeviceIdType.MESH
F32 = jnp.float32
BF16 = jnp.bfloat16


def row_tables():
    owner = np.arange(16)[:, None, None]
    part = np.arange(2)[None, :, None]
    row = np.arange(PAD)[None, None, :]
    y = np.arange(HALF)[None, :]
    tables = []
    for parity in range(2):
        wave = 2 * (ROWS * owner + row) + parity
        valid = np.broadcast_to((wave <= BAND) & (row < ROWS), (16, 2, PAD)).reshape(SIDE, 1)
        waves = np.broadcast_to(wave, (16, 2, PAD)).reshape(SIDE, 1)
        parts = np.broadcast_to(part, (16, 2, PAD)).reshape(SIDE, 1)
        angle = (waves * y % NG) * (2.0 * math.pi / NG)
        tables.append(np.where(valid, np.where(parts == 0, np.cos(angle), -np.sin(angle)), 0.0))
    return np.stack(tables)


def lane_tables():
    index = np.arange(SLAB)
    angle = (index[:, None] * index[None, :] % SLAB) * (2.0 * math.pi / SLAB)
    cos, sin, zero = np.cos(angle), np.sin(angle), np.zeros((SLAB, SLAB))
    pair_forward = np.block(
        [[cos, zero, -sin, zero], [zero, cos, zero, -sin], [sin, zero, cos, zero], [zero, sin, zero, cos]]
    )
    pair_inverse = np.block(
        [[cos, zero, sin, zero], [zero, cos, zero, sin], [-sin, zero, cos, zero], [zero, -sin, zero, cos]]
    )
    twice = []
    for half in range(2):
        real = pair_forward[:, half * SLAB : (half + 1) * SLAB]
        imag = pair_forward[:, (2 + half) * SLAB : (3 + half) * SLAB]
        twice.append(np.concatenate([imag, imag, -real, -real], axis=1))
    return np.stack([twice[0], twice[1], pair_forward, pair_inverse])


def twist_tables():
    first = np.arange(32)[:, None]
    place = (np.arange(LANES) % SLAB)[None, :]
    angle = (first * place) * (2.0 * math.pi / NG)
    return np.stack([np.cos(angle), np.sin(angle)])


def turned(re, im, angle):
    c, s = math.cos(angle), math.sin(angle)
    if abs(s) < 1e-9 and c > 0:
        return re, im
    if abs(c) < 1e-9:
        return (-im, re) if s > 0 else (im, -re)
    if abs(abs(c) - abs(s)) < 1e-9:
        root = math.sqrt(0.5)
        sc, ss = (root if c > 0 else -root), (root if s > 0 else -root)
        if sc == ss:
            return (re - im) * sc, (re + im) * sc
        return (re + im) * sc, (im - re) * sc
    return re * c - im * s, re * s + im * c


def short_transform(res, ims, sign):
    count = len(res)
    if count == 1:
        return res, ims
    er, ei = short_transform(res[0::2], ims[0::2], sign)
    dr, di = short_transform(res[1::2], ims[1::2], sign)
    half = count // 2
    out_r, out_i = [None] * count, [None] * count
    for k in range(half):
        tr, ti = turned(dr[k], di[k], sign * 2.0 * math.pi * k / count)
        out_r[k], out_i[k] = er[k] + tr, ei[k] + ti
        out_r[k + half], out_i[k + half] = er[k] - tr, ei[k] - ti
    return out_r, out_i


def dot(a, b):
    return jnp.dot(a, b, preferred_element_type=F32)


def kernel(
    base_ref,
    tang_ref,
    end_ref,
    tf_hbm,
    ti_hbm,
    lane_ref,
    twist_ref,
    even_ref,
    odd_ref,
    small_ref,
    s1,
    r1,
    s2,
    r2,
    s3,
    r3,
    s4,
    r4,
    gs,
    gr,
    ts,
    tr,
    tb,
    tt,
    tw,
    folded,
    zr,
    zi,
    mult_flow,
    mult_slope,
    mult_decay,
    base_flow,
    product,
    tf_ref,
    ti_ref,
    load_sem,
    send_sem,
    recv_sem,
):
    me = lax.axis_index("spec")
    my_x, my_y, my_core = me // 8, lax.rem(me // 2, 4), lax.rem(me, 2)
    seg = lax.axis_index("tm")
    my_slot = lax.rem(me, 2) * 16 + me // 2
    low = lax.broadcasted_iota(jnp.int32, (1, LANES), 1) < SLAB

    loads = [
        pltpu.make_async_copy(source.at[parity], target.at[parity], load_sem.at[number * 2 + parity])
        for number, (source, target) in enumerate(((tf_hbm, tf_ref), (ti_hbm, ti_ref)))
        for parity in range(2)
    ]
    for load in loads:
        load.start()

    barrier = pltpu.get_barrier_semaphore()

    def greet(d, carry):
        pl.semaphore_signal(barrier, inc=1, device_id={"spec": lax.rem(me + d, SPEC)}, device_id_type=MESH)
        return carry

    for ref in (r1, r2, r3, r4):
        lead = ref.shape[:-2]
        ref[(slice(None),) * len(lead) + (slice(16, 24), slice(None))] = jnp.zeros(lead + (8, LANES), F32)

    lax.fori_loop(1, SPEC, greet, 0)

    def greet_segment(d, carry):
        pl.semaphore_signal(barrier, inc=1, device_id={"tm": lax.rem(seg + d, TM)}, device_id_type=MESH)
        return carry

    lax.fori_loop(1, TM, greet_segment, 0)

    def place(x, y, core):
        return (lax.rem(x, 4) * 4 + lax.rem(y, 4)) * 2 + core

    def slot_of(device):
        return lax.rem(device, 2) * 16 + device // 2

    def start_copy(source, target, out_sem, in_sem, device):
        pltpu.make_async_remote_copy(
            src_ref=source,
            dst_ref=target,
            send_sem=out_sem,
            recv_sem=in_sem,
            device_id={"spec": device},
            device_id_type=MESH,
        ).start()

    def send_core(phase, core, source, target):
        for dx, dy in DIRECT:
            peer = place(my_x + dx, my_y + dy, core)
            start_copy(
                source(peer, slot_of(peer)), target(me, my_slot), send_sem.at[phase], recv_sem.at[phase], peer
            )

    def send_other(phase, source, target):
        peer = place(my_x, my_y, 1 - my_core)
        start_copy(
            source(peer, slot_of(peer)), target(me, my_slot), send_sem.at[phase], recv_sem.at[phase], peer
        )

    def send_all(phase, source, target):
        def step(core, carry):
            send_core(phase, core, source, target)
            return carry

        lax.fori_loop(0, 2, step, 0)
        send_other(phase, source, target)

    def wait_for(sem, phase, ref):
        pltpu.make_async_copy(ref, ref, sem.at[phase]).wait()

    some = pl.ds(0, ROWS)
    front = pl.ds(0, 16)
    back = pl.ds(16, ROWS - 16)
    most = pl.ds(0, SPEC - 1)

    def to_base(origin, slot):
        return r1.at[origin, pl.ds(0, 1), some]

    def to_tangents(origin, slot):
        return r1.at[origin, pl.ds(1, 2), some]

    def to_flow(index):
        return lambda origin, slot: r2.at[index, slot, :, some]

    def to_slope(index, rows):
        return lambda origin, slot: r3.at[index, origin, :, rows]

    def to_evolved(rows):
        return lambda origin, slot: r4.at[slot, :, rows]

    for parity in range(2):
        def fold(half_parity=parity):
            for index, ref in ((0, tang_ref.at[0, 0]), (1, tang_ref.at[0, 1]), (2, base_ref.at[0]), (3, base_ref.at[0])):
                lo, hi = ref[:, :HALF], ref[:, HALF:]
                value = lo + hi if half_parity == 0 else lo - hi
                folded[index * SLAB : (index + 1) * SLAB, :] = value.astype(BF16)

        fold()
        loads[parity].wait()

        def spectrum_rows(step, carry, parity=parity):
            rows = pl.ds(pl.multiple_of(step * 192, 192), 192)
            out = lax.dot_general(
                tf_ref[parity, rows, :], folded[...], (((1,), (1,)), ((), ())), preferred_element_type=F32
            ).reshape(4, 2, PAD, 2 * LANES)
            slots = pl.ds(parity * 16 + step * 4, 4)
            s1[slots, 0] = jnp.where(low[None], out[:, 0, :, LANES:], out[:, 1, :, LANES:])
            s1[slots, 1] = out[:, 0, :, :LANES]
            s1[slots, 2] = out[:, 1, :, :LANES]
            return carry

        lax.fori_loop(0, 4, spectrum_rows, 0)

    pl.semaphore_wait(barrier, SPEC - 1 + TM - 1)
    send_all(0, lambda peer, slot: s1.at[slot, pl.ds(0, 1), some], to_base)
    send_all(1, lambda peer, slot: s1.at[slot, pl.ds(1, 2), some], to_tangents)
    r1[me] = s1[my_slot]

    lane = lax.broadcasted_iota(jnp.int32, (PAD, LANES), 1)
    row = lax.broadcasted_iota(jnp.int32, (PAD, LANES), 0)
    second = 2 * (ROWS * (me // 2) + row) + lax.rem(me, 2)
    second_keep = (second <= BAND) & (row < ROWS)
    second_wave = second.astype(F32)
    low_rows = lane < SLAB
    column = jnp.where(second == 0, 1.0, 2.0)
    to_field = column * (1.0 / float(NG * NG))
    gram_weight = jnp.where(second_keep, column * (1.0 / float(NG) ** 4), 0.0)

    def multipliers(k1, carry):
        first = k1 + 32 * lax.rem(lane, SLAB)
        first = jnp.where(first < HALF, first, first - NG)
        first_wave = first.astype(F32)
        keep = jnp.where(second_keep & (jnp.abs(first) <= BAND), 1.0, 0.0)
        square = first_wave * first_wave + second_wave * second_wave
        inverse = jnp.where(square > 0.0, 1.0 / jnp.maximum(square, 1.0), 0.0)
        decay = keep * jnp.exp(-(visc_scale / BAND**2) * time_step * square)
        mult_flow[k1] = keep * to_field * inverse * jnp.where(low_rows, -second_wave, first_wave)
        mult_decay[k1] = decay
        mult_slope[k1] = (time_step * decay) * jnp.where(
            low_rows,
            first_wave * first_wave - second_wave * second_wave,
            2.0 * first_wave * second_wave,
        )
        return carry

    lax.fori_loop(0, 32, multipliers, 0)

    def first_forward(load, target, start=0, stop=PAD // 8):
        def body(step, carry):
            rows = pl.ds(pl.multiple_of(step * 8, 8), 8)
            pairs = [load(i, rows) for i in range(SPEC)]
            re, im = short_transform([p[0] for p in pairs], [p[1] for p in pairs], -1.0)
            for k1 in range(32):
                c, s = twist_ref[0, k1 : k1 + 1, :], twist_ref[1, k1 : k1 + 1, :]
                target[k1, rows, :LANES] = re[k1] * c + im[k1] * s
                target[k1, rows, LANES:] = im[k1] * c - re[k1] * s
            return carry

        lax.fori_loop(start, stop, body, 0)

    def first_inverse(target, start=0, stop=PAD // 8):
        def body(step, carry):
            rows = pl.ds(pl.multiple_of(step * 8, 8), 8)
            res, ims = [], []
            for k1 in range(32):
                c, s = twist_ref[0, k1 : k1 + 1, :], twist_ref[1, k1 : k1 + 1, :]
                re, im = tw[k1, rows, :LANES], tw[k1, rows, LANES:]
                res.append(re * c - im * s)
                ims.append(im * c + re * s)
            re, im = short_transform(res, ims, 1.0)
            for i in range(SPEC):
                target[i, 0, rows, :] = re[i]
                target[i, 1, rows, :] = im[i]
            return carry

        lax.fori_loop(start, stop, body, 0)

    def chunks(body):
        def step(c, carry):
            body(pl.ds(c * 8, 8))
            return carry

        lax.fori_loop(0, 4, step, 0)

    def flow(source, which, index):
        def body(part):
            spectrum = dot(source[part].reshape(192, 256).astype(BF16), lane_ref[which])
            factor = mult_flow[part].reshape(192, LANES)
            scaled = jnp.concatenate([spectrum[:, :LANES] * factor, spectrum[:, LANES:] * factor], axis=1)
            tw[part] = dot(scaled.astype(BF16), lane_ref[3]).reshape(8, PAD, 256)

        chunks(body)
        first_inverse(s2.at[index])
        send_all(2 + index, lambda peer, slot: s2.at[index, peer, :, some], to_flow(index))
        r2[index, my_slot] = s2[index, me]

    sign = jnp.where(low, 1.0, -1.0)

    def load_base(i, rows):
        value = r1[i, 0, rows, :]
        return value, pltpu.roll(value, SLAB, 1) * sign

    wait_for(recv_sem, 0, r1.at[most, pl.ds(0, 1), some])
    first_forward(load_base, tb)
    flow(tb, 0, 0)
    wait_for(recv_sem, 1, r1.at[most, pl.ds(1, 2), some])
    first_forward(lambda i, rows: (r1[i, 1, rows, :], r1[i, 2, rows, :]), tt)
    flow(tt, 0, 1)
    flow(tt, 1, 2)

    def start_spectrum(part):
        spectrum = dot(tt[part].reshape(192, 256).astype(BF16), lane_ref[2])
        decay = mult_decay[part]
        zr[part] = spectrum[:, :LANES].reshape(8, PAD, LANES) * decay
        zi[part] = spectrum[:, LANES:].reshape(8, PAD, LANES) * decay

    chunks(start_spectrum)

    def second_inverse(ref, body):
        even = ref[pl.ds(0, 16)].reshape(SIDE, LANES).astype(BF16)
        odd = ref[pl.ds(16, 16)].reshape(SIDE, LANES).astype(BF16)

        def step(c, carry):
            rows = pl.ds(pl.multiple_of(c * 256, 256), 256)
            e = dot(ti_ref[0, rows, :], even)
            o = dot(ti_ref[1, rows, :], odd)
            body(c, e + o, e - o)
            return carry

        lax.fori_loop(0, 4, step, 0)

    loads[2].wait()
    loads[3].wait()
    wait_for(recv_sem, 2, r2.at[0, most, :, some])

    def keep_base(c, lower, upper):
        base_flow[pl.ds(pl.multiple_of(c * 256, 256), 256), :] = lower
        base_flow[pl.ds(pl.multiple_of(c * 256 + HALF, 256), 256), :] = upper

    second_inverse(r2.at[0], keep_base)

    def products(b, t):
        straight = b * t
        crossed = b * pltpu.roll(t, SLAB, 1)
        near = jnp.where(low, crossed, straight)
        far = pltpu.roll(jnp.where(low, straight, crossed), SLAB, 1)
        return near + far * sign

    for index in range(2):
        wait_for(recv_sem, 3 + index, r2.at[1 + index, most, :, some])

        def multiply(c, lower, upper):
            rows = pl.ds(pl.multiple_of(c * 256, 256), 256)
            lo = products(base_flow[rows, :], lower)
            hi = products(base_flow[pl.ds(pl.multiple_of(c * 256 + HALF, 256), 256), :], upper)
            product[0, rows, :] = (lo + hi).astype(BF16)
            product[1, rows, :] = (lo - hi).astype(BF16)

        second_inverse(r2.at[1 + index], multiply)

        for parity in range(2):
            def product_rows(step, carry, parity=parity, index=index):
                rows = pl.ds(pl.multiple_of(step * 192, 192), 192)
                out = dot(tf_ref[parity, rows, :], product[parity])
                s3[index, pl.ds(parity * 16 + step * 4, 4)] = out.reshape(4, 2, PAD, LANES)
                return carry

            lax.fori_loop(0, 4, product_rows, 0)

        if index == 0:
            send_all(5, lambda peer, slot: s3.at[0, slot, :, some], to_slope(0, some))
        else:
            send_all(6, lambda peer, slot: s3.at[1, slot, :, front], to_slope(1, front))
            send_all(10, lambda peer, slot: s3.at[1, slot, :, back], to_slope(1, back))
        r3[index, me] = s3[index, my_slot]

    def slope(index, start, count):
        rows = pl.ds(start, count)
        first_forward(
            lambda i, rows: (r3[index, i, 0, rows, :], r3[index, i, 1, rows, :]),
            tb,
            start // 8,
            (start + count) // 8,
        )

        def add_slope(part):
            spectrum = dot(tb[part, rows].reshape(8 * count, 256).astype(BF16), lane_ref[2])
            factor = mult_slope[part, rows].reshape(8 * count, LANES)
            for half, ref in ((0, zr), (1, zi)):
                terms = spectrum[:, half * LANES : (half + 1) * LANES] * factor
                both = terms + pltpu.roll(terms, SLAB, 1)
                both = jnp.where(low, both, 0.0) if index == 0 else jnp.where(low, 0.0, both)
                ref[part, rows] = ref[part, rows] + both.reshape(8, count, LANES)

        chunks(add_slope)

    def evolve(start, count):
        rows = pl.ds(start, count)

        def final_chunk(part):
            scale = jnp.broadcast_to(to_field[None, start : start + count], (8, count, LANES))
            scaled = jnp.concatenate(
                [(ref[part, rows] * scale).reshape(8 * count, LANES) for ref in (zr, zi)], axis=1
            )
            tw[part, rows] = dot(scaled.astype(BF16), lane_ref[3]).reshape(8, count, 256)

        chunks(final_chunk)
        first_inverse(s4, start // 8, (start + count) // 8)

    wait_for(recv_sem, 5, r3.at[0, most, :, some])
    slope(0, 0, PAD)
    wait_for(recv_sem, 6, r3.at[1, most, :, front])
    slope(1, 0, 16)
    evolve(0, 16)
    send_all(7, lambda peer, slot: s4.at[peer, :, front], to_evolved(front))
    wait_for(recv_sem, 10, r3.at[1, most, :, back])
    slope(1, 16, 8)

    def inner(k1, carry):
        squares, crosses = carry
        re, im = zr[k1], zi[k1]
        squares = squares + (re * re + im * im) * gram_weight
        crosses = crosses + (re * pltpu.roll(re, SLAB, 1) + im * pltpu.roll(im, SLAB, 1)) * gram_weight
        return squares, crosses

    nothing = jnp.zeros((PAD, LANES), F32)
    squares, crosses = lax.fori_loop(0, 32, inner, (nothing, nothing))

    def total(x):
        return jnp.sum(jnp.sum(x, axis=0, keepdims=True), axis=1, keepdims=True)

    lane8 = lax.broadcasted_iota(jnp.int32, (8, LANES), 1)

    def spread(first, second, third):
        return jnp.where(lane8 == 0, first, jnp.where(lane8 == 1, second, jnp.where(lane8 == 2, third, 0.0)))

    g00 = total(jnp.where(low_rows, squares, 0.0))
    g11 = total(jnp.where(low_rows, 0.0, squares))
    g01 = total(jnp.where(low_rows, crosses, 0.0))
    gs[...] = spread(g00, g01, g11)

    def share_gram(d, carry):
        start_copy(gs.at[pl.ds(0, 1)], gr.at[me, pl.ds(0, 1)], send_sem.at[8], recv_sem.at[8], lax.rem(me + d, SPEC))
        return carry

    lax.fori_loop(1, SPEC, share_gram, 0)
    gr[me] = gs[...]

    evolve(16, 8)
    send_all(11, lambda peer, slot: s4.at[peer, :, back], to_evolved(back))
    r4[my_slot] = s4[me]


    def pick(values, index):
        return jnp.sum(jnp.where(lane8[:1] == index, values, 0.0), axis=1, keepdims=True)

    wait_for(recv_sem, 8, gr.at[most, pl.ds(0, 1)])
    gram = jnp.sum(gr[:, :1, :], axis=0)
    g00, g01, g11 = pick(gram, 0), pick(gram, 1), pick(gram, 2)
    u00 = jnp.sqrt(g00)
    u01 = g01 / u00
    u11 = jnp.sqrt(g11 - u01 * u01)
    i00, i11 = 1.0 / u00, 1.0 / u11
    i01 = -(i00 * u01) / u11
    i10 = jnp.zeros_like(i00)
    ts[...] = spread(i00, i01, i11)

    def share(d, carry):
        pltpu.make_async_remote_copy(
            src_ref=ts,
            dst_ref=tr.at[seg],
            send_sem=send_sem.at[9],
            recv_sem=recv_sem.at[9],
            device_id={"tm": lax.rem(seg + d, TM)},
            device_id_type=MESH,
        ).start()
        return carry

    lax.fori_loop(1, TM, share, 0)
    tr[seg] = ts[...]
    wait_for(recv_sem, 9, tr.at[pl.ds(0, TM - 1)])
    one, zero = jnp.ones_like(i00), jnp.zeros_like(i00)
    end00, end01, end11 = end_ref[0, 0], end_ref[0, 1], end_ref[1, 1]
    p00, p01, p10, p11 = one, zero, zero, one
    for later in range(TM - 1, -1, -1):
        values = tr[later][:1]
        active = later >= seg
        a00 = jnp.where(active, pick(values, 0), one)
        a01 = jnp.where(active, pick(values, 1), zero)
        a11 = jnp.where(active, pick(values, 2), one)
        a10 = zero
        p00, p01, p10, p11 = (
            a00 * p00 + a01 * p10,
            a00 * p01 + a01 * p11,
            a10 * p00 + a11 * p10,
            a10 * p01 + a11 * p11,
        )
    q00, q01 = p00 * end00, p00 * end01 + p01 * end11
    q10, q11 = p10 * end00, p10 * end01 + p11 * end11
    norm0 = jnp.sqrt(q00 * q00 + q10 * q10)
    norm1 = jnp.sqrt(q01 * q01 + q11 * q11)
    c00, c10, c01, c11 = q00 / norm0, q10 / norm0, q01 / norm1, q11 / norm1
    small = jnp.zeros((8, LANES), F32)
    for number, value in enumerate((c00, c01, c10, c11, i00, i01, i10, i11, jnp.log(u00), jnp.log(u11))):
        small = jnp.where(lane8 == number, value, small)
    small_ref[...] = small

    wait_for(recv_sem, 7, r4.at[most, :, front])
    wait_for(recv_sem, 11, r4.at[most, :, back])
    even_ref[...] = r4[pl.ds(0, 16)].reshape(SIDE, LANES).T.astype(BF16)
    odd_ref[...] = r4[pl.ds(16, 16)].reshape(SIDE, LANES).T.astype(BF16)

    wait_for(send_sem, 0, s1.at[most, pl.ds(0, 1), some])
    wait_for(send_sem, 1, s1.at[most, pl.ds(1, 2), some])
    for index in range(3):
        wait_for(send_sem, 2 + index, s2.at[index, most, :, some])
    wait_for(send_sem, 5, s3.at[0, most, :, some])
    wait_for(send_sem, 6, s3.at[1, most, :, front])
    wait_for(send_sem, 10, s3.at[1, most, :, back])
    wait_for(send_sem, 7, s4.at[most, :, front])
    wait_for(send_sem, 11, s4.at[most, :, back])
    wait_for(send_sem, 8, gr.at[most, pl.ds(0, 1)])
    wait_for(send_sem, 9, tr.at[pl.ds(0, TM - 1)])


def finish(even_ref, odd_ref, small_ref, tf_ref, tang_ref, cov_ref, basis_ref, coef_ref, growth_ref, upper):
    step = pl.program_id(0)
    small = small_ref[:1, :]
    lane = lax.broadcasted_iota(jnp.int32, (1, LANES), 1)

    def pick(index):
        return jnp.sum(jnp.where(lane == index, small, 0.0), axis=1, keepdims=True)

    c00, c01, c10, c11, i00, i01, i10, i11, log0, log1 = [pick(number) for number in range(10)]

    def write(value):
        first, second = value[:SLAB], value[SLAB:]
        basis_ref[0, 0] = first * i00 + second * i10
        basis_ref[0, 1] = first * i01 + second * i11

    @pl.when(step < 2)
    def _():
        e = dot(even_ref[...], tf_ref[0])
        o = dot(odd_ref[...], tf_ref[1])
        upper[step] = e - o
        write(e + o)

    @pl.when(step >= 2)
    def _():
        write(upper[step - 2])

    cov_ref[0, 0] = tang_ref[0, 0] * c00 + tang_ref[0, 1] * c10
    cov_ref[0, 1] = tang_ref[0, 0] * c01 + tang_ref[0, 1] * c11
    across = lax.broadcasted_iota(jnp.int32, (2, 2), 1)
    down = lax.broadcasted_iota(jnp.int32, (2, 2), 0)
    coef_ref[0] = jnp.where(
        down == 0, jnp.where(across == 0, c00, c01), jnp.where(across == 0, c10, c11)
    )
    pair = lax.broadcasted_iota(jnp.int32, (1, 2), 1)
    growth_ref[...] = jnp.where(pair == 0, log0, log1)


def shards(base_flow, tangents, end_matrix):
    rows = row_tables()
    tf = jnp.asarray(rows.astype(ml_dtypes.bfloat16))
    ti = jnp.asarray(np.ascontiguousarray(rows.transpose(0, 2, 1)).astype(ml_dtypes.bfloat16))
    lanes = jnp.asarray(lane_tables().astype(ml_dtypes.bfloat16))
    twist = jnp.asarray(twist_tables().astype(np.float32))
    vmem = pl.BlockSpec(memory_space=pltpu.VMEM)
    smem = pl.BlockSpec(memory_space=pltpu.SMEM)
    hbm = pl.BlockSpec(memory_space=pl.ANY)

    def buffer(*lead):
        return pltpu.VMEM(lead + (PAD, LANES), F32)

    even, odd, small = pl.pallas_call(
        kernel,
        out_shape=(
            pltpu.VMEM((LANES, SIDE), BF16),
            pltpu.VMEM((LANES, SIDE), BF16),
            pltpu.VMEM((8, LANES), F32),
        ),
        in_specs=[vmem, vmem, smem, hbm, hbm, vmem, vmem],
        out_specs=(vmem, vmem, vmem),
        scratch_shapes=[
            buffer(SPEC, 3),
            buffer(SPEC, 3),
            buffer(3, SPEC, 2),
            buffer(3, SPEC, 2),
            buffer(2, SPEC, 2),
            buffer(2, SPEC, 2),
            buffer(SPEC, 2),
            buffer(SPEC, 2),
            pltpu.VMEM((8, LANES), F32),
            pltpu.VMEM((SPEC, 8, LANES), F32),
            pltpu.VMEM((8, LANES), F32),
            pltpu.VMEM((TM, 8, LANES), F32),
            pltpu.VMEM((32, PAD, 256), F32),
            pltpu.VMEM((32, PAD, 256), F32),
            pltpu.VMEM((32, PAD, 256), F32),
            pltpu.VMEM((4 * SLAB, HALF), BF16),
            buffer(32),
            buffer(32),
            buffer(32),
            buffer(32),
            buffer(32),
            pltpu.VMEM((NG, LANES), F32),
            pltpu.VMEM((2, HALF, LANES), BF16),
            pltpu.VMEM((2, SIDE, HALF), BF16),
            pltpu.VMEM((2, HALF, SIDE), BF16),
            pltpu.SemaphoreType.DMA((4,)),
            pltpu.SemaphoreType.DMA((12,)),
            pltpu.SemaphoreType.DMA((12,)),
        ],
        compiler_params=pltpu.CompilerParams(
            collective_id=0, has_side_effects=True, vmem_limit_bytes=56 * 1024 * 1024
        ),
        cost_estimate=pl.CostEstimate(flops=12_000_000_000, bytes_accessed=12_000_000, transcendentals=0),
    )(base_flow, tangents, end_matrix, tf, ti, lanes, twist)

    whole = lambda *shape: pl.BlockSpec(shape, lambda g: (0,) * len(shape))
    wide = pl.BlockSpec((1, K, SLAB, 512), lambda g: (0, 0, 0, g))
    return pl.pallas_call(
        finish,
        grid=(4,),
        out_shape=(
            jax.ShapeDtypeStruct((1, K, SLAB, NG), F32),
            jax.ShapeDtypeStruct((1, K, SLAB, NG), F32),
            jax.ShapeDtypeStruct((1, K, K), F32),
            jax.ShapeDtypeStruct((1, K), F32),
        ),
        in_specs=[
            whole(LANES, SIDE),
            whole(LANES, SIDE),
            whole(8, LANES),
            pl.BlockSpec((2, SIDE, 512), lambda g: (0, 0, jnp.minimum(g, 1))),
            wide,
        ],
        out_specs=(wide, wide, whole(1, K, K), whole(1, K)),
        scratch_shapes=[pltpu.VMEM((2, LANES, 512), F32)],
        compiler_params=pltpu.CompilerParams(vmem_limit_bytes=24 * 1024 * 1024),
        cost_estimate=pl.CostEstimate(flops=400_000_000, bytes_accessed=6_500_000, transcendentals=0),
    )(even, odd, small, tf, tangents)


def solution(mesh):
    in_specs = (P("tm", "spec", None), P("tm", None, "spec", None), P())
    out_specs = (
        P("tm", None, "spec", None),
        P("tm", None, "spec", None),
        P("tm", None, None),
        P("tm", None),
    )
    return jax.shard_map(shards, mesh=mesh, in_specs=in_specs, out_specs=out_specs, check_vma=False)
```

```python
import functools
import math

import jax
import jax.numpy as jnp
import ml_dtypes
import numpy as np
from jax import lax
from jax.experimental import pallas as pl
from jax.experimental.pallas import tpu as pltpu
from jax.sharding import PartitionSpec as P

NG = 2048
HALF = NG // 2
K = 2
SPEC = 32
TM = 8
SLAB = NG // SPEC
BAND = NG // 3
ROWS = 22
PAD = 24
LANES = 128
SIDE = 16 * 2 * PAD

DIRECT = ((2, 2), (1, 2), (2, 1), (3, 2), (2, 3), (2, 0), (0, 2), (1, 1), (3, 3), (1, 3), (3, 1), (1, 0), (0, 1), (3, 0), (0, 3))

time_step = 0.1
visc_scale = 15.0
MESH = pl.DeviceIdType.MESH
F32 = jnp.float32
BF16 = jnp.bfloat16


def row_tables():
    owner = np.arange(16)[:, None, None]
    part = np.arange(2)[None, :, None]
    row = np.arange(PAD)[None, None, :]
    y = np.arange(HALF)[None, :]
    tables = []
    for parity in range(2):
        wave = 2 * (ROWS * owner + row) + parity
        valid = np.broadcast_to((wave <= BAND) & (row < ROWS), (16, 2, PAD)).reshape(SIDE, 1)
        waves = np.broadcast_to(wave, (16, 2, PAD)).reshape(SIDE, 1)
        parts = np.broadcast_to(part, (16, 2, PAD)).reshape(SIDE, 1)
        angle = (waves * y % NG) * (2.0 * math.pi / NG)
        tables.append(np.where(valid, np.where(parts == 0, np.cos(angle), -np.sin(angle)), 0.0))
    return np.stack(tables)


def lane_tables():
    index = np.arange(SLAB)
    angle = (index[:, None] * index[None, :] % SLAB) * (2.0 * math.pi / SLAB)
    cos, sin, zero = np.cos(angle), np.sin(angle), np.zeros((SLAB, SLAB))
    pair_forward = np.block(
        [[cos, zero, -sin, zero], [zero, cos, zero, -sin], [sin, zero, cos, zero], [zero, sin, zero, cos]]
    )
    pair_inverse = np.block(
        [[cos, zero, sin, zero], [zero, cos, zero, sin], [-sin, zero, cos, zero], [zero, -sin, zero, cos]]
    )
    twice = []
    for half in range(2):
        real = pair_forward[:, half * SLAB : (half + 1) * SLAB]
        imag = pair_forward[:, (2 + half) * SLAB : (3 + half) * SLAB]
        twice.append(np.concatenate([imag, imag, -real, -real], axis=1))
    return np.stack([twice[0], twice[1], pair_forward, pair_inverse])


def twist_tables():
    first = np.arange(32)[:, None]
    place = (np.arange(LANES) % SLAB)[None, :]
    angle = (first * place) * (2.0 * math.pi / NG)
    return np.stack([np.cos(angle), np.sin(angle)])


def turned(re, im, angle):
    c, s = math.cos(angle), math.sin(angle)
    if abs(s) < 1e-9 and c > 0:
        return re, im
    if abs(c) < 1e-9:
        return (-im, re) if s > 0 else (im, -re)
    if abs(abs(c) - abs(s)) < 1e-9:
        root = math.sqrt(0.5)
        sc, ss = (root if c > 0 else -root), (root if s > 0 else -root)
        if sc == ss:
            return (re - im) * sc, (re + im) * sc
        return (re + im) * sc, (im - re) * sc
    return re * c - im * s, re * s + im * c


def short_transform(res, ims, sign):
    count = len(res)
    if count == 1:
        return res, ims
    er, ei = short_transform(res[0::2], ims[0::2], sign)
    dr, di = short_transform(res[1::2], ims[1::2], sign)
    half = count // 2
    out_r, out_i = [None] * count, [None] * count
    for k in range(half):
        tr, ti = turned(dr[k], di[k], sign * 2.0 * math.pi * k / count)
        out_r[k], out_i[k] = er[k] + tr, ei[k] + ti
        out_r[k + half], out_i[k + half] = er[k] - tr, ei[k] - ti
    return out_r, out_i


def dot(a, b):
    return jnp.dot(a, b, preferred_element_type=F32)


def kernel(
    base_ref,
    tang_ref,
    end_ref,
    tf_hbm,
    ti_hbm,
    lane_ref,
    twist_ref,
    even_ref,
    odd_ref,
    small_ref,
    s1,
    r1,
    s2,
    r2,
    s3,
    r3,
    s4,
    r4,
    gs,
    gr,
    ts,
    tr,
    tb,
    tt,
    tw,
    folded,
    zr,
    zi,
    mult_flow,
    mult_slope,
    mult_decay,
    base_flow,
    product,
    tf_ref,
    ti_ref,
    load_sem,
    send_sem,
    recv_sem,
):
    me = lax.axis_index("spec")
    my_x, my_y, my_core = me // 8, lax.rem(me // 2, 4), lax.rem(me, 2)
    seg = lax.axis_index("tm")
    my_slot = lax.rem(me, 2) * 16 + me // 2
    low = lax.broadcasted_iota(jnp.int32, (1, LANES), 1) < SLAB

    loads = [
        pltpu.make_async_copy(source.at[parity], target.at[parity], load_sem.at[number * 2 + parity])
        for number, (source, target) in enumerate(((tf_hbm, tf_ref), (ti_hbm, ti_ref)))
        for parity in range(2)
    ]
    for load in loads:
        load.start()

    barrier = pltpu.get_barrier_semaphore()

    def greet(d, carry):
        pl.semaphore_signal(barrier, inc=1, device_id={"spec": lax.rem(me + d, SPEC)}, device_id_type=MESH)
        return carry

    for ref in (r1, r2, r3, r4):
        lead = ref.shape[:-2]
        ref[(slice(None),) * len(lead) + (slice(16, 24), slice(None))] = jnp.zeros(lead + (8, LANES), F32)

    lax.fori_loop(1, SPEC, greet, 0)

    def greet_segment(d, carry):
        pl.semaphore_signal(barrier, inc=1, device_id={"tm": lax.rem(seg + d, TM)}, device_id_type=MESH)
        return carry

    lax.fori_loop(1, TM, greet_segment, 0)

    def place(x, y, core):
        return (lax.rem(x, 4) * 4 + lax.rem(y, 4)) * 2 + core

    def slot_of(device):
        return lax.rem(device, 2) * 16 + device // 2

    def start_copy(source, target, out_sem, in_sem, device):
        pltpu.make_async_remote_copy(
            src_ref=source,
            dst_ref=target,
            send_sem=out_sem,
            recv_sem=in_sem,
            device_id={"spec": device},
            device_id_type=MESH,
        ).start()

    def send_core(phase, core, source, target):
        for dx, dy in DIRECT:
            peer = place(my_x + dx, my_y + dy, core)
            start_copy(
                source(peer, slot_of(peer)), target(me, my_slot), send_sem.at[phase], recv_sem.at[phase], peer
            )

    def send_other(phase, source, target):
        peer = place(my_x, my_y, 1 - my_core)
        start_copy(
            source(peer, slot_of(peer)), target(me, my_slot), send_sem.at[phase], recv_sem.at[phase], peer
        )

    def send_all(phase, source, target):
        def step(core, carry):
            send_core(phase, core, source, target)
            return carry

        lax.fori_loop(0, 2, step, 0)
        send_other(phase, source, target)

    def wait_for(sem, phase, ref):
        pltpu.make_async_copy(ref, ref, sem.at[phase]).wait()

    some = pl.ds(0, ROWS)
    front = pl.ds(0, 16)
    back = pl.ds(16, ROWS - 16)
    most = pl.ds(0, SPEC - 1)

    def to_base(origin, slot):
        return r1.at[origin, pl.ds(0, 1), some]

    def to_tangents(origin, slot):
        return r1.at[origin, pl.ds(1, 2), some]

    def to_flow(index):
        return lambda origin, slot: r2.at[index, slot, :, some]

    def to_slope(index, rows):
        return lambda origin, slot: r3.at[index, origin, :, rows]

    def to_evolved(rows):
        return lambda origin, slot: r4.at[slot, :, rows]

    for parity in range(2):
        def fold(half_parity=parity):
            for index, ref in ((0, tang_ref.at[0, 0]), (1, tang_ref.at[0, 1]), (2, base_ref.at[0]), (3, base_ref.at[0])):
                lo, hi = ref[:, :HALF], ref[:, HALF:]
                value = lo + hi if half_parity == 0 else lo - hi
                folded[index * SLAB : (index + 1) * SLAB, :] = value.astype(BF16)

        fold()
        loads[parity].wait()

        def spectrum_rows(step, carry, parity=parity):
            rows = pl.ds(pl.multiple_of(step * 192, 192), 192)
            out = lax.dot_general(
                tf_ref[parity, rows, :], folded[...], (((1,), (1,)), ((), ())), preferred_element_type=F32
            ).reshape(4, 2, PAD, 2 * LANES)
            slots = pl.ds(parity * 16 + step * 4, 4)
            s1[slots, 0] = jnp.where(low[None], out[:, 0, :, LANES:], out[:, 1, :, LANES:])
            s1[slots, 1] = out[:, 0, :, :LANES]
            s1[slots, 2] = out[:, 1, :, :LANES]
            return carry

        lax.fori_loop(0, 4, spectrum_rows, 0)

    pl.semaphore_wait(barrier, SPEC - 1 + TM - 1)
    send_all(0, lambda peer, slot: s1.at[slot, pl.ds(0, 1), some], to_base)
    send_all(1, lambda peer, slot: s1.at[slot, pl.ds(1, 2), some], to_tangents)
    r1[me] = s1[my_slot]

    lane = lax.broadcasted_iota(jnp.int32, (PAD, LANES), 1)
    row = lax.broadcasted_iota(jnp.int32, (PAD, LANES), 0)
    second = 2 * (ROWS * (me // 2) + row) + lax.rem(me, 2)
    second_keep = (second <= BAND) & (row < ROWS)
    second_wave = second.astype(F32)
    low_rows = lane < SLAB
    column = jnp.where(second == 0, 1.0, 2.0)
    to_field = column * (1.0 / float(NG * NG))
    gram_weight = jnp.where(second_keep, column * (1.0 / float(NG) ** 4), 0.0)

    def multipliers(k1, carry):
        first = k1 + 32 * lax.rem(lane, SLAB)
        first = jnp.where(first < HALF, first, first - NG)
        first_wave = first.astype(F32)
        keep = jnp.where(second_keep & (jnp.abs(first) <= BAND), 1.0, 0.0)
        square = first_wave * first_wave + second_wave * second_wave
        inverse = jnp.where(square > 0.0, 1.0 / jnp.maximum(square, 1.0), 0.0)
        decay = keep * jnp.exp(-(visc_scale / BAND**2) * time_step * square)
        mult_flow[k1] = keep * to_field * inverse * jnp.where(low_rows, -second_wave, first_wave)
        mult_decay[k1] = decay
        mult_slope[k1] = (time_step * decay) * jnp.where(
            low_rows,
            first_wave * first_wave - second_wave * second_wave,
            2.0 * first_wave * second_wave,
        )
        return carry

    lax.fori_loop(0, 32, multipliers, 0)

    def first_forward(load, target, start=0, stop=PAD // 8):
        def body(step, carry):
            rows = pl.ds(pl.multiple_of(step * 8, 8), 8)
            pairs = [load(i, rows) for i in range(SPEC)]
            re, im = short_transform([p[0] for p in pairs], [p[1] for p in pairs], -1.0)
            for k1 in range(32):
                c, s = twist_ref[0, k1 : k1 + 1, :], twist_ref[1, k1 : k1 + 1, :]
                target[k1, rows, :LANES] = re[k1] * c + im[k1] * s
                target[k1, rows, LANES:] = im[k1] * c - re[k1] * s
            return carry

        lax.fori_loop(start, stop, body, 0)

    def first_inverse(target, start=0, stop=PAD // 8):
        def body(step, carry):
            rows = pl.ds(pl.multiple_of(step * 8, 8), 8)
            res, ims = [], []
            for k1 in range(32):
                c, s = twist_ref[0, k1 : k1 + 1, :], twist_ref[1, k1 : k1 + 1, :]
                re, im = tw[k1, rows, :LANES], tw[k1, rows, LANES:]
                res.append(re * c - im * s)
                ims.append(im * c + re * s)
            re, im = short_transform(res, ims, 1.0)
            for i in range(SPEC):
                target[i, 0, rows, :] = re[i]
                target[i, 1, rows, :] = im[i]
            return carry

        lax.fori_loop(start, stop, body, 0)

    def chunks(body):
        def step(c, carry):
            body(pl.ds(c * 8, 8))
            return carry

        lax.fori_loop(0, 4, step, 0)

    def flow(source, which, index):
        def body(part):
            spectrum = dot(source[part].reshape(192, 256).astype(BF16), lane_ref[which])
            factor = mult_flow[part].reshape(192, LANES)
            scaled = jnp.concatenate([spectrum[:, :LANES] * factor, spectrum[:, LANES:] * factor], axis=1)
            tw[part] = dot(scaled.astype(BF16), lane_ref[3]).reshape(8, PAD, 256)

        chunks(body)
        first_inverse(s2.at[index])
        send_all(2 + index, lambda peer, slot: s2.at[index, peer, :, some], to_flow(index))
        r2[index, my_slot] = s2[index, me]

    sign = jnp.where(low, 1.0, -1.0)

    def load_base(i, rows):
        value = r1[i, 0, rows, :]
        return value, pltpu.roll(value, SLAB, 1) * sign

    wait_for(recv_sem, 0, r1.at[most, pl.ds(0, 1), some])
    first_forward(load_base, tb)
    flow(tb, 0, 0)
    wait_for(recv_sem, 1, r1.at[most, pl.ds(1, 2), some])
    first_forward(lambda i, rows: (r1[i, 1, rows, :], r1[i, 2, rows, :]), tt)
    flow(tt, 0, 1)
    flow(tt, 1, 2)

    def start_spectrum(part):
        spectrum = dot(tt[part].reshape(192, 256).astype(BF16), lane_ref[2])
        decay = mult_decay[part]
        zr[part] = spectrum[:, :LANES].reshape(8, PAD, LANES) * decay
        zi[part] = spectrum[:, LANES:].reshape(8, PAD, LANES) * decay

    chunks(start_spectrum)

    def second_inverse(ref, body):
        even = ref[pl.ds(0, 16)].reshape(SIDE, LANES).astype(BF16)
        odd = ref[pl.ds(16, 16)].reshape(SIDE, LANES).astype(BF16)

        def step(c, carry):
            rows = pl.ds(pl.multiple_of(c * 256, 256), 256)
            e = dot(ti_ref[0, rows, :], even)
            o = dot(ti_ref[1, rows, :], odd)
            body(c, e + o, e - o)
            return carry

        lax.fori_loop(0, 4, step, 0)

    loads[2].wait()
    loads[3].wait()
    wait_for(recv_sem, 2, r2.at[0, most, :, some])

    def keep_base(c, lower, upper):
        base_flow[pl.ds(pl.multiple_of(c * 256, 256), 256), :] = lower
        base_flow[pl.ds(pl.multiple_of(c * 256 + HALF, 256), 256), :] = upper

    second_inverse(r2.at[0], keep_base)

    def products(b, t):
        straight = b * t
        crossed = b * pltpu.roll(t, SLAB, 1)
        near = jnp.where(low, crossed, straight)
        far = pltpu.roll(jnp.where(low, straight, crossed), SLAB, 1)
        return near + far * sign

    for index in range(2):
        wait_for(recv_sem, 3 + index, r2.at[1 + index, most, :, some])

        def multiply(c, lower, upper):
            rows = pl.ds(pl.multiple_of(c * 256, 256), 256)
            lo = products(base_flow[rows, :], lower)
            hi = products(base_flow[pl.ds(pl.multiple_of(c * 256 + HALF, 256), 256), :], upper)
            product[0, rows, :] = (lo + hi).astype(BF16)
            product[1, rows, :] = (lo - hi).astype(BF16)

        second_inverse(r2.at[1 + index], multiply)

        for parity in range(2):
            def product_rows(step, carry, parity=parity, index=index):
                rows = pl.ds(pl.multiple_of(step * 192, 192), 192)
                out = dot(tf_ref[parity, rows, :], product[parity])
                s3[index, pl.ds(parity * 16 + step * 4, 4)] = out.reshape(4, 2, PAD, LANES)
                return carry

            lax.fori_loop(0, 4, product_rows, 0)

        if index == 0:
            send_all(5, lambda peer, slot: s3.at[0, slot, :, some], to_slope(0, some))
        else:
            send_all(6, lambda peer, slot: s3.at[1, slot, :, front], to_slope(1, front))
            send_all(10, lambda peer, slot: s3.at[1, slot, :, back], to_slope(1, back))
        r3[index, me] = s3[index, my_slot]

    def slope(index, start, count):
        rows = pl.ds(start, count)
        first_forward(
            lambda i, rows: (r3[index, i, 0, rows, :], r3[index, i, 1, rows, :]),
            tb,
            start // 8,
            (start + count) // 8,
        )

        def add_slope(part):
            spectrum = dot(tb[part, rows].reshape(8 * count, 256).astype(BF16), lane_ref[2])
            factor = mult_slope[part, rows].reshape(8 * count, LANES)
            for half, ref in ((0, zr), (1, zi)):
                terms = spectrum[:, half * LANES : (half + 1) * LANES] * factor
                both = terms + pltpu.roll(terms, SLAB, 1)
                both = jnp.where(low, both, 0.0) if index == 0 else jnp.where(low, 0.0, both)
                ref[part, rows] = ref[part, rows] + both.reshape(8, count, LANES)

        chunks(add_slope)

    def evolve(start, count):
        rows = pl.ds(start, count)

        def final_chunk(part):
            scale = jnp.broadcast_to(to_field[None, start : start + count], (8, count, LANES))
            scaled = jnp.concatenate(
                [(ref[part, rows] * scale).reshape(8 * count, LANES) for ref in (zr, zi)], axis=1
            )
            tw[part, rows] = dot(scaled.astype(BF16), lane_ref[3]).reshape(8, count, 256)

        chunks(final_chunk)
        first_inverse(s4, start // 8, (start + count) // 8)

    wait_for(recv_sem, 5, r3.at[0, most, :, some])
    slope(0, 0, PAD)
    wait_for(recv_sem, 6, r3.at[1, most, :, front])
    slope(1, 0, 16)
    evolve(0, 16)
    send_all(7, lambda peer, slot: s4.at[peer, :, front], to_evolved(front))
    wait_for(recv_sem, 10, r3.at[1, most, :, back])
    slope(1, 16, 8)

    def inner(k1, carry):
        squares, crosses = carry
        re, im = zr[k1], zi[k1]
        squares = squares + (re * re + im * im) * gram_weight
        crosses = crosses + (re * pltpu.roll(re, SLAB, 1) + im * pltpu.roll(im, SLAB, 1)) * gram_weight
        return squares, crosses

    nothing = jnp.zeros((PAD, LANES), F32)
    squares, crosses = lax.fori_loop(0, 32, inner, (nothing, nothing))

    def total(x):
        return jnp.sum(jnp.sum(x, axis=0, keepdims=True), axis=1, keepdims=True)

    lane8 = lax.broadcasted_iota(jnp.int32, (8, LANES), 1)

    def spread(first, second, third):
        return jnp.where(lane8 == 0, first, jnp.where(lane8 == 1, second, jnp.where(lane8 == 2, third, 0.0)))

    g00 = total(jnp.where(low_rows, squares, 0.0))
    g11 = total(jnp.where(low_rows, 0.0, squares))
    g01 = total(jnp.where(low_rows, crosses, 0.0))
    gs[...] = spread(g00, g01, g11)

    def share_gram(d, carry):
        start_copy(gs.at[pl.ds(0, 1)], gr.at[me, pl.ds(0, 1)], send_sem.at[8], recv_sem.at[8], lax.rem(me + d, SPEC))
        return carry

    lax.fori_loop(1, SPEC, share_gram, 0)
    gr[me] = gs[...]

    evolve(16, 8)
    send_all(11, lambda peer, slot: s4.at[peer, :, back], to_evolved(back))
    r4[my_slot] = s4[me]


    def pick(values, index):
        return jnp.sum(jnp.where(lane8[:1] == index, values, 0.0), axis=1, keepdims=True)

    wait_for(recv_sem, 8, gr.at[most, pl.ds(0, 1)])
    gram = jnp.sum(gr[:, :1, :], axis=0)
    g00, g01, g11 = pick(gram, 0), pick(gram, 1), pick(gram, 2)
    u00 = jnp.sqrt(g00)
    u01 = g01 / u00
    u11 = jnp.sqrt(g11 - u01 * u01)
    i00, i11 = 1.0 / u00, 1.0 / u11
    i01 = -(i00 * u01) / u11
    i10 = jnp.zeros_like(i00)
    ts[...] = spread(i00, i01, i11)

    def share(d, carry):
        pltpu.make_async_remote_copy(
            src_ref=ts.at[pl.ds(0, 1)],
            dst_ref=tr.at[seg, pl.ds(0, 1)],
            send_sem=send_sem.at[9],
            recv_sem=recv_sem.at[9],
            device_id={"tm": lax.rem(seg + d, TM)},
            device_id_type=MESH,
        ).start()
        return carry

    lax.fori_loop(1, TM, share, 0)
    tr[seg] = ts[...]
    wait_for(recv_sem, 9, tr.at[pl.ds(0, TM - 1), pl.ds(0, 1)])
    one, zero = jnp.ones_like(i00), jnp.zeros_like(i00)
    end00, end01, end11 = end_ref[0, 0], end_ref[0, 1], end_ref[1, 1]
    p00, p01, p10, p11 = one, zero, zero, one
    for later in range(TM - 1, -1, -1):
        values = tr[later, :1, :]
        active = later >= seg
        a00 = jnp.where(active, pick(values, 0), one)
        a01 = jnp.where(active, pick(values, 1), zero)
        a11 = jnp.where(active, pick(values, 2), one)
        a10 = zero
        p00, p01, p10, p11 = (
            a00 * p00 + a01 * p10,
            a00 * p01 + a01 * p11,
            a10 * p00 + a11 * p10,
            a10 * p01 + a11 * p11,
        )
    q00, q01 = p00 * end00, p00 * end01 + p01 * end11
    q10, q11 = p10 * end00, p10 * end01 + p11 * end11
    norm0 = jnp.sqrt(q00 * q00 + q10 * q10)
    norm1 = jnp.sqrt(q01 * q01 + q11 * q11)
    c00, c10, c01, c11 = q00 / norm0, q10 / norm0, q01 / norm1, q11 / norm1
    small = jnp.zeros((8, LANES), F32)
    for number, value in enumerate((c00, c01, c10, c11, i00, i01, i10, i11, jnp.log(u00), jnp.log(u11))):
        small = jnp.where(lane8 == number, value, small)
    small_ref[...] = small

    wait_for(recv_sem, 7, r4.at[most, :, front])
    wait_for(recv_sem, 11, r4.at[most, :, back])
    even_ref[...] = r4[pl.ds(0, 16)].reshape(SIDE, LANES).T.astype(BF16)
    odd_ref[...] = r4[pl.ds(16, 16)].reshape(SIDE, LANES).T.astype(BF16)

    wait_for(send_sem, 0, s1.at[most, pl.ds(0, 1), some])
    wait_for(send_sem, 1, s1.at[most, pl.ds(1, 2), some])
    for index in range(3):
        wait_for(send_sem, 2 + index, s2.at[index, most, :, some])
    wait_for(send_sem, 5, s3.at[0, most, :, some])
    wait_for(send_sem, 6, s3.at[1, most, :, front])
    wait_for(send_sem, 10, s3.at[1, most, :, back])
    wait_for(send_sem, 7, s4.at[most, :, front])
    wait_for(send_sem, 11, s4.at[most, :, back])
    wait_for(send_sem, 8, gr.at[most, pl.ds(0, 1)])
    wait_for(send_sem, 9, tr.at[pl.ds(0, TM - 1), pl.ds(0, 1)])


def finish(even_ref, odd_ref, small_ref, tf_ref, tang_ref, cov_ref, basis_ref, coef_ref, growth_ref, upper):
    step = pl.program_id(0)
    small = small_ref[:1, :]
    lane = lax.broadcasted_iota(jnp.int32, (1, LANES), 1)

    def pick(index):
        return jnp.sum(jnp.where(lane == index, small, 0.0), axis=1, keepdims=True)

    c00, c01, c10, c11, i00, i01, i10, i11, log0, log1 = [pick(number) for number in range(10)]

    def write(value):
        first, second = value[:SLAB], value[SLAB:]
        basis_ref[0, 0] = first * i00 + second * i10
        basis_ref[0, 1] = first * i01 + second * i11

    @pl.when(step == 0)
    def _():
        e = dot(even_ref[...], tf_ref[0])
        o = dot(odd_ref[...], tf_ref[1])
        upper[...] = e - o
        write(e + o)

    @pl.when(step == 1)
    def _():
        write(upper[...])

    cov_ref[0, 0] = tang_ref[0, 0] * c00 + tang_ref[0, 1] * c10
    cov_ref[0, 1] = tang_ref[0, 0] * c01 + tang_ref[0, 1] * c11
    across = lax.broadcasted_iota(jnp.int32, (2, 2), 1)
    down = lax.broadcasted_iota(jnp.int32, (2, 2), 0)
    coef_ref[0] = jnp.where(
        down == 0, jnp.where(across == 0, c00, c01), jnp.where(across == 0, c10, c11)
    )
    pair = lax.broadcasted_iota(jnp.int32, (1, 2), 1)
    growth_ref[...] = jnp.where(pair == 0, log0, log1)


def shards(base_flow, tangents, end_matrix):
    rows = row_tables()
    tf = jnp.asarray(rows.astype(ml_dtypes.bfloat16))
    ti = jnp.asarray(np.ascontiguousarray(rows.transpose(0, 2, 1)).astype(ml_dtypes.bfloat16))
    lanes = jnp.asarray(lane_tables().astype(ml_dtypes.bfloat16))
    twist = jnp.asarray(twist_tables().astype(np.float32))
    vmem = pl.BlockSpec(memory_space=pltpu.VMEM)
    smem = pl.BlockSpec(memory_space=pltpu.SMEM)
    hbm = pl.BlockSpec(memory_space=pl.ANY)

    def buffer(*lead):
        return pltpu.VMEM(lead + (PAD, LANES), F32)

    even, odd, small = pl.pallas_call(
        kernel,
        out_shape=(
            pltpu.VMEM((LANES, SIDE), BF16),
            pltpu.VMEM((LANES, SIDE), BF16),
            pltpu.VMEM((8, LANES), F32),
        ),
        in_specs=[vmem, vmem, smem, hbm, hbm, vmem, vmem],
        out_specs=(vmem, vmem, vmem),
        scratch_shapes=[
            buffer(SPEC, 3),
            buffer(SPEC, 3),
            buffer(3, SPEC, 2),
            buffer(3, SPEC, 2),
            buffer(2, SPEC, 2),
            buffer(2, SPEC, 2),
            buffer(SPEC, 2),
            buffer(SPEC, 2),
            pltpu.VMEM((8, LANES), F32),
            pltpu.VMEM((SPEC, 8, LANES), F32),
            pltpu.VMEM((8, LANES), F32),
            pltpu.VMEM((TM, 8, LANES), F32),
            pltpu.VMEM((32, PAD, 256), F32),
            pltpu.VMEM((32, PAD, 256), F32),
            pltpu.VMEM((32, PAD, 256), F32),
            pltpu.VMEM((4 * SLAB, HALF), BF16),
            buffer(32),
            buffer(32),
            buffer(32),
            buffer(32),
            buffer(32),
            pltpu.VMEM((NG, LANES), F32),
            pltpu.VMEM((2, HALF, LANES), BF16),
            pltpu.VMEM((2, SIDE, HALF), BF16),
            pltpu.VMEM((2, HALF, SIDE), BF16),
            pltpu.SemaphoreType.DMA((4,)),
            pltpu.SemaphoreType.DMA((12,)),
            pltpu.SemaphoreType.DMA((12,)),
        ],
        compiler_params=pltpu.CompilerParams(
            collective_id=0, has_side_effects=True, vmem_limit_bytes=56 * 1024 * 1024
        ),
        cost_estimate=pl.CostEstimate(flops=12_000_000_000, bytes_accessed=12_000_000, transcendentals=0),
    )(base_flow, tangents, end_matrix, tf, ti, lanes, twist)

    whole = lambda *shape: pl.BlockSpec(shape, lambda g: (0,) * len(shape))
    wide = pl.BlockSpec((1, K, SLAB, HALF), lambda g: (0, 0, 0, g))
    return pl.pallas_call(
        finish,
        grid=(2,),
        out_shape=(
            jax.ShapeDtypeStruct((1, K, SLAB, NG), F32),
            jax.ShapeDtypeStruct((1, K, SLAB, NG), F32),
            jax.ShapeDtypeStruct((1, K, K), F32),
            jax.ShapeDtypeStruct((1, K), F32),
        ),
        in_specs=[
            whole(LANES, SIDE),
            whole(LANES, SIDE),
            whole(8, LANES),
            whole(2, SIDE, HALF),
            wide,
        ],
        out_specs=(wide, wide, whole(1, K, K), whole(1, K)),
        scratch_shapes=[pltpu.VMEM((LANES, HALF), F32)],
        compiler_params=pltpu.CompilerParams(vmem_limit_bytes=24 * 1024 * 1024),
        cost_estimate=pl.CostEstimate(flops=400_000_000, bytes_accessed=6_500_000, transcendentals=0),
    )(even, odd, small, tf, tangents)


def solution(mesh):
    in_specs = (P("tm", "spec", None), P("tm", None, "spec", None), P())
    out_specs = (
        P("tm", None, "spec", None),
        P("tm", None, "spec", None),
        P("tm", None, None),
        P("tm", None),
    )
    return jax.shard_map(shards, mesh=mesh, in_specs=in_specs, out_specs=out_specs, check_vma=False)
```
